128 devices in a mesh: stream: 32 (over z, y, core), azim: 4 (over x).
Axes of the slice: x: 4, y: 4, z: 4, core: 2. Of those that a mesh axis runs over, the one named last changes fastest.
Arguments:
- history: float32 [3, 3, 64, 262144], P(None, None, None, ('stream', 'azim')), may hold values from -6 to 6
- block_ids: int32 [16384], P(('stream', 'azim')), may hold values from 0 to 16383, as said below
- len_axial: float32 [128], replicated, may hold values from 0.7 to 17.5, as said below
- len_azim: float32 [16], replicated, may hold values from 0.8 to 2.4
- len_radial: float32 [128], replicated, may hold values from 0.8 to 2.4
- solid: int32 [128, 16, 128], P('stream', 'azim'), may hold values 0 or 1
Outputs:
- velocity: float32 [3, 4, 4, 4, 128, 16, 128], P(None, None, None, None, 'stream', 'azim')
- pressure: float32 [4, 4, 4, 128, 16, 128], P(None, None, None, 'stream', 'azim')
The draws below stay inside these ranges and needn't reach their ends.
Inputs may be any that keep to these rules, and one draw needn't show every extreme that they name: `block_ids`: A permutation of 0 .. 16383. Block id g goes to the device of linear index g // 128 (flow index major), which lies in the sender's azimuthal sector. A device sends at most 2 blocks to any other device; in every draw some device sends 2 blocks to some other, and some device receives 2 blocks from every other device of its sector. `len_axial`: Positive.
All inputs are finite; a program needn't handle non-finite values. No bound on the sum of `solid` on one device may be relied on, other than what follows from the above.
Results may differ from the reference program's by a relative error of at most 0.0001.
Values sent between devices are 32-bit elements; how exact they have to be, the bound alone decides.
No kernel may reach another device: no remote copies, remote signals or barrier semaphores. Data moves between devices by JAX's collectives and lax.ppermute only.
A program may use at most 128 MiB of HBM per device.

```python
import math
import jax
import jax.numpy as jnp
import numpy as np
from jax import lax

EX = 4
EY = 4
EZ = 128
BE = 16
CAP = 2
ITERS = 2
NBLK = 128
NBLOCKS = 16384
NEX = 128
NEY = 16
N_STREAM = 32
N_AZIM = 4


def draw_block_ids(key, part):
    slab_count = NEX // EX
    sector_count = NEY // EY
    blocks = NBLK
    raw = jax.random.randint(jax.random.fold_in(key, 11), (sector_count, slab_count, slab_count), 0, CAP + 1)
    upper = jnp.triu(raw, 1)
    counts = upper + jnp.transpose(upper, (0, 2, 1))
    source = jnp.arange(slab_count)[None, :, None]
    target = jnp.arange(slab_count)[None, None, :]
    stride = jax.random.randint(jax.random.fold_in(key, 12), (sector_count, 1, 1), 1, slab_count)
    distance = (target - source) % slab_count
    counts = jnp.where((distance == stride) | (distance == slab_count - stride), CAP, counts)
    center = jax.random.randint(jax.random.fold_in(key, 13), (sector_count, 1, 1), 0, slab_count)
    counts = jnp.where((source == center) | (target == center), CAP, counts)
    counts = jnp.where(source == target, 0, counts)
    staying = blocks - jnp.sum(counts, axis=2, keepdims=True)
    counts = counts + jnp.where(source == target, staying, 0)
    out_end = jnp.cumsum(counts, axis=2)
    out_begin = out_end - counts
    in_begin = jnp.cumsum(counts, axis=1) - counts
    position = jnp.arange(blocks)[None, None, :]
    goes_to = jnp.sum((out_end[:, :, :, None] <= position[:, :, None, :]).astype(jnp.int32), axis=2)
    ranked = position - jnp.take_along_axis(out_begin, goes_to, axis=2)
    arrive = jnp.take_along_axis(in_begin, goes_to, axis=2) + ranked
    scores_new = jax.random.randint(jax.random.fold_in(key, 14), (sector_count, slab_count, blocks), 0, 1 << 20) * blocks + position
    shuffle_new = jnp.argsort(scores_new, axis=2).reshape(sector_count, slab_count * blocks)
    new_slot = jnp.take_along_axis(shuffle_new, (goes_to * blocks + arrive).reshape(sector_count, slab_count * blocks), axis=1)
    new_slot = new_slot.reshape(sector_count, slab_count, blocks)
    sector_index = jnp.arange(sector_count)[:, None, None]
    global_id = (goes_to * sector_count + sector_index) * blocks + new_slot
    scores_old = jax.random.randint(jax.random.fold_in(key, 15), (sector_count, slab_count, blocks), 0, 1 << 20) * blocks + position
    shuffle_old = jnp.argsort(scores_old, axis=2)
    placed = jnp.take_along_axis(global_id, shuffle_old, axis=2)
    return jnp.transpose(placed, (1, 0, 2)).reshape(-1).astype(jnp.int32)


def draw_len_axial(key, part):
    fraction = jnp.arange(NEX).astype(jnp.float32) / NEX
    rough = jnp.exp(jax.random.uniform(key, (NEX,), jnp.float32, math.log(0.6), math.log(1.6)))
    return 1.2 * jnp.exp(fraction * math.log(3.0)) * rough


def with_ends(values, stream_key, smallest, largest):
    longest = values.shape.index(max(values.shape))
    spots = []
    for shift in (0, 1):
        where = [jax.random.randint(jax.random.fold_in(stream_key, axis), (), 0, length) for axis, length in enumerate(values.shape)]
        where[longest] = (where[longest] + shift) % values.shape[longest]
        spots.append(tuple(where))
    return values.at[spots[0]].set(smallest).at[spots[1]].set(largest)


def block_levels(rng, shape, shards, smallest, high):
    factor_of = 1.0
    for dim, shards_of in shards:
        steps = jax.random.uniform(jax.random.fold_in(jax.random.fold_in(rng, 6), dim), (shards_of,), jnp.float32, smallest / len(shards), high / len(shards))
        factor_of = factor_of * jnp.repeat(jnp.exp(steps), shape[dim] // shards_of).reshape((-1,) + (1,) * (len(shape) - 1 - dim))
    return factor_of


def gaussian(rng, dims, deviation, bound, shards=(), kind=jnp.bfloat16):
    values = jax.random.normal(rng, dims, jnp.float32) * deviation
    if len(shards) > 0:
        values = block_levels(rng, dims, shards, -0.22, 0.18) * values
    return jnp.clip(values, min=-bound, max=bound).astype(kind)


def setup_inputs(seed: int = 0) -> dict:
    keys = jax.random.split(jax.random.key(seed), 7)
    history = gaussian(keys[0], (3, 3, 64, NBLOCKS * BE), 1.0, 6.0, ((3, 128),), jnp.float32)
    block_ids = draw_block_ids(jax.random.fold_in(keys[6], 71), 0)
    len_axial = draw_len_axial(jax.random.fold_in(keys[6], 71), 0)
    len_azim = jnp.clip(jnp.exp(jax.random.uniform(keys[3], (NEY,), jnp.float32, math.log(0.8), math.log(2.4))), 0.8, 2.4)
    len_radial = jnp.clip(jnp.exp(jax.random.uniform(keys[4], (EZ,), jnp.float32, math.log(0.8), math.log(2.4))), 0.8, 2.4)
    solid = with_ends((jax.random.randint(keys[5], (NEX, NEY, EZ), 0, 4) < 1).astype(jnp.int32), jax.random.fold_in(keys[5], 1), 0, 1)
    return dict(history=history, block_ids=block_ids, len_axial=len_axial, len_azim=len_azim, len_radial=len_radial, solid=solid)


DT = 0.01
PENALTY = 100.0
HIGH = lax.Precision.HIGHEST
FORWARD = ('ia,kabc...->kibc...', 'ib,kabc...->kaic...', 'ic,kabc...->kabi...')
BACKWARD = ('ai,kabc...->kibc...', 'bi,kabc...->kaic...', 'ci,kabc...->kabi...')

def node_tables():
    root = 1.0 / math.sqrt(5.0)
    points = np.array([-1.0, -root, root, 1.0])
    weights = np.array([1.0 / 6.0, 5.0 / 6.0, 5.0 / 6.0, 1.0 / 6.0])
    legendre = (5.0 * points ** 3 - 3.0 * points) / 2.0
    slope = np.zeros((4, 4))
    for first in range(4):
        for second in range(4):
            if first != second:
                slope[first, second] = legendre[first] / (legendre[second] * (points[first] - points[second]))
    slope[0, 0] = -3.0
    slope[3, 3] = 3.0
    return (jnp.asarray(slope, dtype=jnp.float32), jnp.asarray(weights, dtype=jnp.float32))

def along(field, axis_pick, backward):
    slope, _ = node_tables()
    form = BACKWARD[axis_pick] if backward else FORWARD[axis_pick]
    return jnp.einsum(form, slope, field, precision=HIGH)

def weight_cube(trailing):
    _, weights = node_tables()
    cube = weights[:, None, None] * weights[None, :, None] * weights[None, None, :]
    return cube.reshape((4, 4, 4) + (1,) * trailing)

def predictor(history, scales):
    newest, middle, oldest = (history[0], history[1], history[2])
    extrap = 3.0 * newest - 3.0 * middle + oldest
    advect = jnp.zeros_like(extrap)
    for axis_pick in range(3):
        advect = advect + extrap[axis_pick] * (scales[axis_pick] * along(extrap, axis_pick, False))
    return 3.0 * newest - 1.5 * middle + oldest / 3.0 - DT * advect

def load_elements(predicted, scales):
    trailing = predicted.ndim - 4
    jacobian = 1.0 / (scales[0] * scales[1] * scales[2])
    spread = jnp.zeros_like(predicted[0])
    for axis_pick in range(3):
        spread = spread + scales[axis_pick] * along(predicted[axis_pick:axis_pick + 1], axis_pick, False)[0]
    return -(jacobian * weight_cube(trailing)) * spread

def stiffness(field, scales):
    trailing = field.ndim - 3
    jacobian = 1.0 / (scales[0] * scales[1] * scales[2])
    cube = weight_cube(trailing)
    lifted = field[None]
    total = jnp.zeros_like(lifted)
    for axis_pick in range(3):
        factor = scales[axis_pick] * scales[axis_pick] * jacobian * cube
        total = total + along(factor * along(lifted, axis_pick, False), axis_pick, True)
    return total[0]

def gradient(field, scales):
    lifted = field[None]
    return jnp.concatenate([scales[axis_pick] * along(lifted, axis_pick, False) for axis_pick in range(3)], axis=0)

def split_axis(nodal, axis):
    count = (nodal.shape[axis] - 1) // 3
    shape = nodal.shape[:axis] + (count, 3) + nodal.shape[axis + 1:]
    head = lax.slice_in_dim(nodal, 0, 3 * count, axis=axis).reshape(shape)
    pieces = [lax.index_in_dim(head, node, axis + 1, keepdims=False) for node in range(3)]
    pieces.append(lax.slice_in_dim(nodal, 3, 3 * count + 1, stride=3, axis=axis))
    return jnp.stack(pieces, axis=axis)

def join_axis(elements, axis):
    count = elements.shape[axis + 1]
    pieces = [lax.index_in_dim(elements, node, axis, keepdims=False) for node in range(4)]
    zero = jnp.zeros_like(pieces[0])
    shape = pieces[0].shape[:axis] + (3 * count,) + pieces[0].shape[axis + 1:]
    main = jnp.stack(pieces[:3], axis=axis + 1).reshape(shape)
    last = jnp.stack([pieces[3], zero, zero], axis=axis + 1).reshape(shape)
    single = jnp.zeros(shape[:axis] + (1,) + shape[axis + 1:], elements.dtype)
    triple = jnp.zeros(shape[:axis] + (3,) + shape[axis + 1:], elements.dtype)
    main = jnp.concatenate([main, single], axis=axis)
    last = lax.slice_in_dim(jnp.concatenate([triple, last], axis=axis), 0, 3 * count + 1, axis=axis)
    return main + last

def to_elements(nodal):
    split = split_axis(split_axis(split_axis(nodal, 0), 2), 4)
    return jnp.transpose(split, (0, 2, 4, 1, 3, 5))

def from_elements(elements):
    spread = jnp.transpose(elements, (0, 3, 1, 4, 2, 5))
    return join_axis(join_axis(join_axis(spread, 4), 2), 0)

def extend(unique):
    wrapped = jnp.concatenate([unique, unique[:, :1]], axis=1)
    wrapped = jnp.concatenate([wrapped, jnp.zeros((1,) + wrapped.shape[1:], wrapped.dtype)], axis=0)
    return jnp.concatenate([wrapped, jnp.zeros(wrapped.shape[:2] + (1,), wrapped.dtype)], axis=2)

def fold(nodal):
    inside = nodal[:-1, :, :-1]
    core = inside[:, :-1]
    return core.at[:, 0].add(inside[:, -1])

def operate(unique, scales):
    return fold(from_elements(stiffness(to_elements(extend(unique)), scales)))

def reference(history, block_ids, len_axial, len_azim, len_radial, solid):
    count = block_ids.shape[0]
    order = jnp.zeros((count,), jnp.int32).at[block_ids].set(jnp.arange(count, dtype=jnp.int32))
    blocks = history.reshape(3, 3, 64, count, BE)
    moved = jnp.take(blocks, order, axis=3)
    moved = moved.reshape(3, 3, 4, 4, 4, N_STREAM, N_AZIM, EX, EY, EZ)
    moved = jnp.transpose(moved, (0, 1, 2, 3, 4, 5, 7, 6, 8, 9)).reshape(3, 3, 4, 4, 4, NEX, NEY, EZ)
    scales = (2.0 / len_axial[:, None, None], 2.0 / len_azim[None, :, None], 2.0 / len_radial[None, None, :])
    numer = predictor(moved, scales)
    predicted = numer / (11.0 / 6.0 + DT * PENALTY * solid.astype(jnp.float32))
    load = fold(from_elements(load_elements(predicted, scales)))
    solution = jnp.zeros_like(load)
    residual = load
    direction = load
    norm_now = jnp.sum(residual * residual)
    for step in range(ITERS):
        image = operate(direction, scales)
        alpha = norm_now / jnp.sum(direction * image)
        solution = solution + alpha * direction
        residual = residual - alpha * image
        norm_next = jnp.sum(residual * residual)
        direction = residual + norm_next / norm_now * direction
        norm_now = norm_next
    pressure = to_elements(extend(solution))
    velocity = predicted - gradient(pressure, scales)
    return (velocity, pressure)
```

```python
import functools
import math

import jax
import jax.numpy as jnp
import numpy as np
from jax import lax
from jax.experimental import pallas as pl
from jax.experimental.pallas import tpu as pltpu
from jax.sharding import PartitionSpec as P

CAP = 2
DT = 0.01
PENALTY = 100.0
VMEM_LIMIT = 40 * 1024 * 1024
F32 = jnp.float32


def node_tables():
    root = 1.0 / math.sqrt(5.0)
    points = np.array([-1.0, -root, root, 1.0])
    weights = np.array([1.0 / 6.0, 5.0 / 6.0, 5.0 / 6.0, 1.0 / 6.0])
    legendre = (5.0 * points**3 - 3.0 * points) / 2.0
    slope = np.zeros((4, 4))
    for first in range(4):
        for second in range(4):
            if first != second:
                slope[first, second] = legendre[first] / (
                    legendre[second] * (points[first] - points[second])
                )
    slope[0, 0] = -3.0
    slope[3, 3] = 3.0
    return slope, weights


SLOPE, WEIGHT = node_tables()
STIFF = SLOPE.T @ np.diag(WEIGHT) @ SLOPE
EDGE = float(WEIGHT[0])

ROWS = 8
BLOCK_ROWS = 24
PEER_ROWS = CAP * BLOCK_ROWS + ROWS


def iotas():
    lane = lax.broadcasted_iota(jnp.int32, (ROWS, 128), 1)
    sub = lax.broadcasted_iota(jnp.int32, (ROWS, 128), 0)
    return lane, sub


def lanes(x, shift):
    shift %= 128
    return pltpu.roll(x, shift, 1) if shift else x


def subs(x, shift):
    shift %= ROWS
    return pltpu.roll(x, shift, 0) if shift else x


def combine(coefs, values):
    total = None
    for coef, value in zip(coefs, values):
        coef = float(coef)
        if coef == 0.0:
            continue
        term = coef * value
        total = term if total is None else total + term
    return total


def choose(key, values):
    result = values[0]
    for at in range(1, len(values)):
        result = jnp.where(key == at, values[at], result)
    return result


def swap_groups(tiles, group):
    turned = [lanes(tile, 16 * t) for t, tile in enumerate(tiles)]
    result = []
    for g in range(8):
        mixed = choose((group - g) & 7, turned)
        result.append(lanes(mixed, -16 * g))
    return result


def pack_kernel(ids, len_axial, len_azim, len_radial, hist, send, keep, count, table):
    sectors = lax.axis_size("azim")
    me = lax.axis_index("stream")
    step = pl.program_id(0)
    columns = hist.shape[1] // 128
    lane, sub = iotas()
    group = lane >> 4

    @pl.when(step == 0)
    def _():
        for t in range(send.shape[0] // PEER_ROWS):
            count[t] = 0
            send[pl.ds(t * PEER_ROWS + CAP * BLOCK_ROWS, ROWS), :] = jnp.zeros((ROWS, 128), F32)
        whole = jnp.broadcast_to(len_radial[...], (ROWS, 128))
        rows = choose(sub, [lanes(whole, -16 * z) for z in range(8)])
        rows = jnp.where(group == 0, rows, 0.0)
        for shift in (16, 32, 64):
            rows = rows + lanes(rows, shift)
        table[...] = rows

    def pattern(low, high):
        return jnp.where(sub < 4, F32(low), F32(high))

    def column(at, carry):
        offset = pl.multiple_of(at * 128, 128)

        def level(which, comp, t):
            return hist[pl.ds((which * 3 + comp) * 64 + 8 * t, ROWS), pl.ds(offset, 128)]

        places = []
        axial = azim = radial = None
        for piece in range(8):
            p = (step * columns + at) * 8 + piece
            ident = ids[p]
            owner = ident >> 7
            slot = ident & 127
            flow = owner // sectors
            sector = owner - flow * sectors
            places.append((flow, slot))
            one_axial = len_axial[flow * 4 + (slot >> 5)]
            one_azim = len_azim[sector * 4 + ((slot >> 3) & 3)]
            one_radial = table[pl.ds(slot & 7, 1), :]
            if piece == 0:
                axial = jnp.full((ROWS, 128), one_axial, F32)
                azim = jnp.full((ROWS, 128), one_azim, F32)
                radial = jnp.broadcast_to(one_radial, (ROWS, 128))
            else:
                axial = jnp.where(group == piece, one_axial, axial)
                azim = jnp.where(group == piece, one_azim, azim)
                radial = jnp.where(group == piece, one_radial, radial)
        scales = [(-2.0 * DT) / length for length in (axial, azim, radial)]

        extrap = [
            [3.0 * level(0, comp, t) - 3.0 * level(1, comp, t) + level(2, comp, t) for t in range(8)]
            for comp in range(3)
        ]
        wind = [[scales[axis] * extrap[axis][t] for t in range(8)] for axis in range(3)]
        c_at = sub & 3
        spin = []
        for k in range(4):
            value = jnp.zeros((ROWS, 128), F32)
            for c in range(4):
                value = jnp.where(c_at == c, F32(SLOPE[c, (c + k) % 4]), value)
            spin.append(value)
        same = [[pattern(SLOPE[2 * p, 2 * o], SLOPE[2 * p + 1, 2 * o + 1]) for o in range(2)] for p in range(2)]
        cross = [[pattern(SLOPE[2 * p, 2 * o + 1], SLOPE[2 * p + 1, 2 * o]) for o in range(2)] for p in range(2)]
        packed = []
        for comp in range(3):
            ue = extrap[comp]
            flipped = [subs(ue[t], 4) for t in range(8)]
            tiles = []
            for t in range(8):
                a, half = t // 2, t % 2
                along_a = combine(SLOPE[a], [ue[2 * o + half] for o in range(4)])
                along_b = (
                    same[half][0] * ue[2 * a]
                    + cross[half][0] * flipped[2 * a]
                    + same[half][1] * ue[2 * a + 1]
                    + cross[half][1] * flipped[2 * a + 1]
                )
                along_c = spin[0] * ue[t]
                for k in range(1, 4):
                    moved = jnp.where(c_at + k < 4, subs(ue[t], -k), subs(ue[t], 4 - k))
                    along_c = along_c + spin[k] * moved
                advect = wind[0][t] * along_a + wind[1][t] * along_b + wind[2][t] * along_c
                base = (
                    3.0 * level(0, comp, t)
                    - 1.5 * level(1, comp, t)
                    + level(2, comp, t) * F32(1.0 / 3.0)
                )
                tiles.append(base + advect)
            packed.append(swap_groups(tiles, group))

        for piece in range(8):
            flow, slot = places[piece]
            rank = count[flow]

            @pl.when(flow != me)
            def _(flow=flow, slot=slot, rank=rank, piece=piece):
                count[flow] = rank + 1
                row = pl.multiple_of(flow * PEER_ROWS + rank * BLOCK_ROWS, ROWS)
                for comp in range(3):
                    send[pl.ds(row + comp * ROWS, ROWS), :] = packed[comp][piece]
                mark = pl.multiple_of(flow * PEER_ROWS + CAP * BLOCK_ROWS, ROWS)
                old = send[pl.ds(mark, ROWS), :]
                here = (sub == 0) & (lane == CAP * me + rank)
                send[pl.ds(mark, ROWS), :] = jnp.where(here, (slot + 1).astype(F32), old)

            @pl.when(flow == me)
            def _(slot=slot, piece=piece):
                row = pl.multiple_of(slot * BLOCK_ROWS, ROWS)
                for comp in range(3):
                    keep[pl.ds(row + comp * ROWS, ROWS), :] = packed[comp][piece]

        return carry

    lax.fori_loop(0, columns, column, 0)


def at(a, b, c, h):
    return pl.ds((a * 16 + b * 4 + c) * 16 + h * ROWS, ROWS)


def join_radial(line, lane):
    first = line[0] + jnp.where(lane == 0, 0.0, lanes(line[3], 1))
    last = jnp.where(lane == 127, 0.0, lanes(first, -1))
    return [first, line[1], line[2], last]


def join_azim(ref, sub):
    ey = sub & 3
    for a in range(4):
        for c in range(4):
            for h in range(2):
                low = ref[at(a, 0, c, h), :]
                high = ref[at(a, 3, c, h), :]
                ref[at(a, 0, c, h), :] = low + jnp.where(ey == 0, 0.0, subs(high, 1))
                ref[at(a, 3, c, h), :] = high + jnp.where(ey == 3, 0.0, subs(low, -1))


def join_axial(ref, b, c, sub):
    top = sub < 4
    low = [ref[at(0, b, c, h), :] for h in range(2)]
    high = [ref[at(3, b, c, h), :] for h in range(2)]
    low_turned = [subs(x, 4) for x in low]
    high_turned = [subs(x, 4) for x in high]
    new_low = [
        low[0] + jnp.where(top, 0.0, high_turned[0]),
        low[1] + jnp.where(top, high_turned[0], high_turned[1]),
    ]
    new_high = [
        high[0] + jnp.where(top, low_turned[0], low_turned[1]),
        high[1] + jnp.where(top, low_turned[1], 0.0),
    ]
    return new_low, new_high


def lengths(len_axial, len_azim, len_radial, sub):
    slab = lax.axis_index("stream")
    sector = lax.axis_index("azim")
    columns, rows = len_axial.shape[0], len_azim.shape[0]
    x0, y0 = slab * 4, sector * 4
    top = sub < 4
    axial = [jnp.where(top, len_axial[x0 + 2 * h], len_axial[x0 + 2 * h + 1]) for h in range(2)]
    azim = choose(sub & 3, [jnp.full((ROWS, 128), len_azim[y0 + k], F32) for k in range(4)])
    radial = jnp.broadcast_to(len_radial[...], (ROWS, 128))
    before = len_axial[jnp.maximum(x0 - 1, 0)]
    after = len_axial[jnp.minimum(x0 + 4, columns - 1)]
    below = len_azim[lax.rem(y0 + rows - 1, rows)]
    above = len_azim[lax.rem(y0 + 4, rows)]
    return axial, azim, radial, (before, after, below, above)


def load_kernel(
    len_axial, len_azim, len_radial, solid, arrived, keep, pred, part, up, down, blocks, marks, marks_s, sem, sem2
):
    lane, sub = iotas()
    group = lane >> 4
    peers = arrived.shape[0] // PEER_ROWS
    fetch = pltpu.make_async_copy(keep, blocks, sem)
    fetch.start()
    total = None
    for t in range(peers):
        tile = arrived[pl.ds(t * PEER_ROWS + CAP * BLOCK_ROWS, ROWS), :]
        total = tile if total is None else total + tile
    marks[...] = total.astype(jnp.int32)
    scalars = pltpu.make_async_copy(marks, marks_s, sem2)
    scalars.start()
    scalars.wait()
    fetch.wait()

    def place(n, carry):
        label = marks_s[0, n]

        @pl.when(label > 0)
        def _():
            target = pl.multiple_of((label - 1) * BLOCK_ROWS, ROWS)
            source = pl.multiple_of((n // CAP) * PEER_ROWS + (n % CAP) * BLOCK_ROWS, ROWS)
            for comp in range(3):
                blocks[pl.ds(target + comp * ROWS, ROWS), :] = arrived[
                    pl.ds(source + comp * ROWS, ROWS), :
                ]

        return carry

    lax.fori_loop(0, peers * CAP, place, 0)

    def unpack(j, carry):
        for comp in range(3):
            tiles = [
                blocks[pl.ds(pl.multiple_of((j * 8 + g) * BLOCK_ROWS, ROWS) + comp * ROWS, ROWS), :]
                for g in range(8)
            ]
            for t, tile in enumerate(swap_groups(tiles, group)):
                pred[pl.ds(comp * 1024 + 8 * t * 16 + j, ROWS, stride=16), :] = tile
        return carry

    lax.fori_loop(0, 16, unpack, 0)

    axial, azim, radial, _ = lengths(len_axial, len_azim, len_radial, sub)
    inverse = [
        1.0 / (F32(11.0 / 6.0) + F32(DT * PENALTY) * solid[pl.ds(h * ROWS, ROWS), :].astype(F32))
        for h in range(2)
    ]

    def scaled(comp, a, b, c, h):
        spot = pl.ds(comp * 1024 + (a * 16 + b * 4 + c) * 16 + h * ROWS, ROWS)
        value = pred[spot, :] * inverse[h]
        pred[spot, :] = value
        return value

    area = [
        [0.25 * azim * radial for h in range(2)],
        [0.25 * axial[h] * radial for h in range(2)],
        [0.25 * axial[h] * azim for h in range(2)],
    ]
    for h in range(2):
        for b in range(4):
            for c in range(4):
                line = [scaled(0, a, b, c, h) for a in range(4)]
                for a in range(4):
                    part[at(a, b, c, h), :] = area[0][h] * combine(SLOPE[a], line)
        for a in range(4):
            for c in range(4):
                line = [scaled(1, a, b, c, h) for b in range(4)]
                for b in range(4):
                    part[at(a, b, c, h), :] += area[1][h] * combine(SLOPE[b], line)
        for a in range(4):
            for b in range(4):
                line = [scaled(2, a, b, c, h) for c in range(4)]
                line = [
                    float(-WEIGHT[a] * WEIGHT[b] * WEIGHT[c])
                    * (part[at(a, b, c, h), :] + area[2][h] * combine(SLOPE[c], line))
                    for c in range(4)
                ]
                for c, value in enumerate(join_radial(line, lane)):
                    part[at(a, b, c, h), :] = value
    join_azim(part, sub)
    top = sub < 4
    for b in range(4):
        for c in range(4):
            low, high = join_axial(part, b, c, sub)
            for h in range(2):
                part[at(0, b, c, h), :] = low[h]
                part[at(3, b, c, h), :] = high[h]
            inner = [[part[at(a, b, c, h), :] for a in (1, 2)] for h in range(2)]
            spot = pl.ds((b * 4 + c) * ROWS, ROWS)
            normal = combine(STIFF[3], [low[1], *inner[1], high[1]])
            up[spot, :] = jnp.where(top, subs(high[1], 4), normal)
            normal = combine(STIFF[0], [low[0], *inner[0], high[0]])
            down[spot, :] = jnp.where(top, low[0], subs(normal, 4))


def axial_kernel(part, below, above, field, normals, up, down):
    lane, sub = iotas()
    top = sub < 4
    slab = lax.axis_index("stream")
    first = jnp.where(slab == 0, F32(0.0), F32(1.0))
    last = jnp.where(slab == lax.axis_size("stream") - 1, F32(0.0), F32(1.0))
    for b in range(4):
        for c in range(4):
            spot = pl.ds((b * 4 + c) * ROWS, ROWS)
            low = part[at(0, b, c, 0), :]
            high = part[at(3, b, c, 1), :]
            under, over = below[spot, :], above[spot, :]
            normals[spot, :] = jnp.where(
                top,
                subs(under, 4) + float(STIFF[3, 3]) * low,
                over + float(STIFF[0, 0]) * high,
            )
            field[at(0, b, c, 0), :] = low + jnp.where(top, first * under, 0.0)
            field[at(3, b, c, 1), :] = jnp.where(top, high, last * (high + subs(over, 4)))
            field[at(0, b, c, 1), :] = part[at(0, b, c, 1), :]
            field[at(3, b, c, 0), :] = part[at(3, b, c, 0), :]
            for a in (1, 2):
                for h in range(2):
                    field[at(a, b, c, h), :] = part[at(a, b, c, h), :]
    ey = sub & 3
    for a in range(4):
        for c in range(4):
            spot = pl.ds((a * 4 + c) * ROWS, ROWS)
            line = [[field[at(a, b, c, h), :] for b in range(4)] for h in range(2)]
            normal = [combine(STIFF[3], line[h]) for h in range(2)]
            up[spot, :] = choose(
                ey, [subs(normal[1], -3), subs(normal[0], -2), subs(line[1][3], -1), line[0][3]]
            )
            normal = [combine(STIFF[0], line[h]) for h in range(2)]
            down[spot, :] = choose(
                ey, [line[0][0], subs(line[1][0], 1), subs(normal[0], 2), subs(normal[1], 3)]
            )
    spot = pl.ds(16 * ROWS, ROWS)
    edge = [normals[pl.ds((12 + c) * ROWS, ROWS), :] for c in range(4)]
    up[spot, :] = choose(ey, [subs(edge[3], -3), subs(edge[2], -2), subs(edge[1], -1), edge[0]])
    edge = [normals[pl.ds(c * ROWS, ROWS), :] for c in range(4)]
    down[spot, :] = choose(ey, [edge[0], subs(edge[1], 1), subs(edge[2], 2), subs(edge[3], 3)])


def image_kernel(
    len_axial, len_azim, len_radial, part, normals_in, below, above, field, image, sums, normals, sides
):
    lane, sub = iotas()
    top = sub < 4
    ey = sub & 3
    slab = lax.axis_index("stream")
    first = jnp.where(slab == 0, F32(0.0), F32(1.0))
    last = jnp.where(slab == lax.axis_size("stream") - 1, F32(0.0), F32(1.0))
    for a in range(4):
        for c in range(4):
            spot = pl.ds((a * 4 + c) * ROWS, ROWS)
            under, over = below[spot, :], above[spot, :]
            under_face = [subs(under, -3), subs(under, -2)]
            under_normal = [subs(under, -1), under]
            over_face = [subs(over, 3), subs(over, 2)]
            over_normal = [subs(over, 1), over]
            for h in range(2):
                low = part[at(a, 0, c, h), :]
                high = part[at(a, 3, c, h), :]
                sides[pl.ds(((a * 4 + c) * 2 + h) * ROWS, ROWS), :] = jnp.where(
                    ey == 0,
                    under_normal[h] + float(STIFF[3, 3]) * low,
                    over_normal[h] + float(STIFF[0, 0]) * high,
                )
                field[at(a, 0, c, h), :] = low + jnp.where(ey == 0, under_face[h], 0.0)
                field[at(a, 3, c, h), :] = high + jnp.where(ey == 3, over_face[h], 0.0)
                for b in (1, 2):
                    field[at(a, b, c, h), :] = part[at(a, b, c, h), :]
    under, over = below[pl.ds(16 * ROWS, ROWS), :], above[pl.ds(16 * ROWS, ROWS), :]
    for c in range(4):
        spot = pl.ds(c * ROWS, ROWS)
        normals[spot, :] = normals_in[spot, :] + jnp.where(ey == 0, subs(under, c - 3), 0.0)
        spot = pl.ds((12 + c) * ROWS, ROWS)
        normals[spot, :] = normals_in[spot, :] + jnp.where(ey == 3, subs(over, 3 - c), 0.0)
        for b in (1, 2):
            spot = pl.ds((b * 4 + c) * ROWS, ROWS)
            normals[spot, :] = normals_in[spot, :]

    axial, azim, radial, (before, after, beneath, beyond) = lengths(
        len_axial, len_azim, len_radial, sub
    )
    zero = jnp.zeros((ROWS, 128), F32)
    rx = [2.0 / axial[h] for h in range(2)]
    ry = 2.0 / azim
    rz = 2.0 / radial
    qz = 0.5 * radial
    qx = [[0.5 * axial[h] for a in range(4)] for h in range(2)]
    before_v, after_v = jnp.full((ROWS, 128), before, F32), jnp.full((ROWS, 128), after, F32)
    beneath_v, beyond_v = jnp.full((ROWS, 128), beneath, F32), jnp.full((ROWS, 128), beyond, F32)
    own_x = [qx[h][0] for h in range(2)]
    qx[0][0] = own_x[0] + jnp.where(top, first * 0.5 * before_v, 0.0)
    qx[1][3] = own_x[1] + jnp.where(top, 0.0, last * 0.5 * after_v)
    ghost_x = [jnp.where(top, first * 2.0 / before_v, 0.0), jnp.where(top, 0.0, last * 2.0 / after_v)]
    own_y = 0.5 * azim
    qy = [
        own_y + jnp.where(ey == 0, 0.5 * beneath_v, 0.0),
        own_y,
        own_y,
        own_y + jnp.where(ey == 3, 0.5 * beyond_v, 0.0),
    ]
    ghost_y = [jnp.where(ey == 0, 2.0 / beneath_v, 0.0), zero, zero, jnp.where(ey == 3, 2.0 / beyond_v, 0.0)]

    for h in range(2):
        factor = [rx[h] * qz * qy[b] for b in range(4)]
        extra = [ghost_x[h] * qz * qy[b] for b in range(4)]
        edge_a = 0 if h == 0 else 3
        for b in range(4):
            for c in range(4):
                line = [field[at(a, b, c, h), :] for a in range(4)]
                for a in range(4):
                    value = factor[b] * combine(STIFF[a], line)
                    if a == edge_a:
                        value = value + extra[b] * normals[pl.ds((b * 4 + c) * ROWS, ROWS), :]
                    image[at(a, b, c, h), :] = float(WEIGHT[b] * WEIGHT[c]) * value
        for a in range(4):
            factor_a = ry * qz * qx[h][a]
            extra_a = [ghost_y[b] * qz * qx[h][a] for b in range(4)]
            for c in range(4):
                line = [field[at(a, b, c, h), :] for b in range(4)]
                side = sides[pl.ds(((a * 4 + c) * 2 + h) * ROWS, ROWS), :]
                for b in range(4):
                    value = factor_a * combine(STIFF[b], line)
                    if b in (0, 3):
                        value = value + extra_a[b] * side
                    image[at(a, b, c, h), :] += float(WEIGHT[a] * WEIGHT[c]) * value
        for a in range(4):
            for b in range(4):
                factor_ab = (float(WEIGHT[a] * WEIGHT[b]) * rz) * qx[h][a] * qy[b]
                line = [field[at(a, b, c, h), :] for c in range(4)]
                line = [
                    image[at(a, b, c, h), :] + factor_ab * combine(STIFF[c], line)
                    for c in range(4)
                ]
                for c, value in enumerate(join_radial(line, lane)):
                    image[at(a, b, c, h), :] = value
    join_azim(image, sub)
    outlet = jnp.where(top, 1.0, last)
    for b in range(4):
        for c in range(4):
            low, high = join_axial(image, b, c, sub)
            high[1] = high[1] * outlet
            for h in range(2):
                image[at(0, b, c, h), :] = low[h]
                image[at(3, b, c, h), :] = high[h]

    load_load = load_image = image_image = zero
    for h in range(2):
        for a in range(3):
            for b in range(3):
                for c in range(3):
                    one, two = field[at(a, b, c, h), :], image[at(a, b, c, h), :]
                    load_load = load_load + one * one
                    load_image = load_image + one * two
                    image_image = image_image + two * two
    energy = zero
    for h in range(2):
        along = [zero, zero, zero]
        for m in range(4):
            for n in range(4):
                weight = float(WEIGHT[m] * WEIGHT[n])
                lines = (
                    [image[at(k, m, n, h), :] for k in range(4)],
                    [image[at(m, k, n, h), :] for k in range(4)],
                    [image[at(m, n, k, h), :] for k in range(4)],
                )
                for axis, line in enumerate(lines):
                    dot = None
                    for k in range(4):
                        term = line[k] * combine(STIFF[k], line)
                        dot = term if dot is None else dot + term
                    along[axis] = along[axis] + weight * dot
        energy = (
            energy
            + rx[h] * own_y * qz * along[0]
            + ry * own_x[h] * qz * along[1]
            + rz * own_x[h] * own_y * along[2]
        )
    row = zero
    for k, value in enumerate((load_load, load_image, image_image, energy)):
        value = jnp.sum(jnp.sum(value, axis=0, keepdims=True), axis=1, keepdims=True)
        row = jnp.where(lane == k, jnp.broadcast_to(value, (ROWS, 128)), row)
    for k in range(sums.shape[0] // ROWS):
        sums[pl.ds(k * ROWS, ROWS), :] = row


def final_kernel(len_axial, len_azim, len_radial, sums, field, image, pred, velocity, pressure):
    lane, sub = iotas()
    total = sums[pl.ds(0, ROWS), :]
    for k in range(1, sums.shape[0] // ROWS):
        total = total + sums[pl.ds(k * ROWS, ROWS), :]
    total = jnp.broadcast_to(jnp.sum(total, axis=0, keepdims=True), (ROWS, 128))
    s0, s1, s2, s3 = (
        jnp.broadcast_to(
            jnp.sum(jnp.where(lane == k, total, 0.0), axis=1, keepdims=True), (ROWS, 128)
        )
        for k in range(4)
    )
    alpha = s0 / s1
    ratio = s2 / s1
    grown = alpha * ratio
    energy = alpha * (s3 - s2 * ratio)
    second = s0 * (grown - 1.0) / (alpha * energy)
    of_load = alpha + second * grown
    of_image = -(second * alpha)

    axial, azim, radial, _ = lengths(len_axial, len_azim, len_radial, sub)
    for h in range(2):
        for a in range(4):
            for b in range(4):
                for c in range(4):
                    spot = at(a, b, c, h)
                    pressure[spot, :] = of_load * field[spot, :] + of_image * image[spot, :]
    for h in range(2):
        scales = (2.0 / axial[h], 2.0 / azim, 2.0 / radial)
        for m in range(4):
            for n in range(4):
                lines = (
                    [(k, m, n) for k in range(4)],
                    [(m, k, n) for k in range(4)],
                    [(m, n, k) for k in range(4)],
                )
                for axis, line in enumerate(lines):
                    values = [pressure[at(*node, h), :] for node in line]
                    for k, (a, b, c) in enumerate(line):
                        spot = pl.ds(axis * 1024 + (a * 16 + b * 4 + c) * 16 + h * ROWS, ROWS)
                        velocity[spot, :] = pred[spot, :] - scales[axis] * combine(
                            SLOPE[k], values
                        )


SMEM = pl.BlockSpec(memory_space=pltpu.SMEM)
VMEM = pl.BlockSpec(memory_space=pltpu.VMEM)
ANY = pl.BlockSpec(memory_space=pl.ANY)


def array(rows, kind=F32):
    return jax.ShapeDtypeStruct((rows, 128), kind)


def call(kernel, ins, outs, scratch, name):
    return pl.pallas_call(
        kernel,
        out_shape=outs,
        in_specs=ins,
        out_specs=[VMEM] * len(outs),
        scratch_shapes=scratch,
        compiler_params=pltpu.CompilerParams(vmem_limit_bytes=VMEM_LIMIT),
        name=name,
    )


def around(axis, value, shift):
    count = lax.axis_size(axis)
    return lax.ppermute(value, axis, [(i, (i + shift) % count) for i in range(count)])


def body(history, block_ids, len_axial, len_azim, len_radial, solid):
    slabs, sectors = lax.axis_size("stream"), lax.axis_size("azim")
    radial = len_radial.reshape(1, 128)
    geometry = (len_axial, len_azim, radial)
    geometry_specs = [SMEM, SMEM, VMEM]
    steps = 4
    hist = history.reshape(576, history.shape[3])
    send, keep = pl.pallas_call(
        pack_kernel,
        grid=(steps,),
        out_shape=[array(slabs * PEER_ROWS), array(128 * BLOCK_ROWS)],
        in_specs=[
            SMEM,
            SMEM,
            SMEM,
            pl.BlockSpec((1, 128), lambda i: (0, 0)),
            pl.BlockSpec((576, hist.shape[1] // steps), lambda i: (0, i)),
        ],
        out_specs=[
            pl.BlockSpec((slabs * PEER_ROWS, 128), lambda i: (0, 0)),
            pl.BlockSpec((128 * BLOCK_ROWS, 128), lambda i: (0, 0)),
        ],
        scratch_shapes=[pltpu.SMEM((slabs,), jnp.int32), pltpu.VMEM((ROWS, 128), F32)],
        compiler_params=pltpu.CompilerParams(
            vmem_limit_bytes=VMEM_LIMIT, dimension_semantics=("arbitrary",)
        ),
        name="pack",
    )(block_ids, len_axial, len_azim, radial, hist)
    arrived = lax.all_to_all(
        send.reshape(slabs, PEER_ROWS, 128), "stream", split_axis=0, concat_axis=0, tiled=True
    ).reshape(slabs * PEER_ROWS, 128)
    pred, part, up, down = call(
        load_kernel,
        geometry_specs + [VMEM, VMEM, ANY],
        [array(3 * 1024), array(1024), array(128), array(128)],
        [
            pltpu.VMEM((128 * BLOCK_ROWS, 128), F32),
            pltpu.VMEM((ROWS, 128), jnp.int32),
            pltpu.SMEM((ROWS, 128), jnp.int32),
            pltpu.SemaphoreType.DMA(()),
            pltpu.SemaphoreType.DMA(()),
        ],
        "load",
    )(*geometry, solid.reshape(16, 128), arrived, keep)
    below, above = around("stream", up, 1), around("stream", down, -1)
    part, normals, up, down = call(
        axial_kernel,
        [VMEM] * 3,
        [array(1024), array(128), array(136), array(136)],
        [],
        "axial_faces",
    )(part, below, above)
    below, above = around("azim", up, 1), around("azim", down, -1)
    field, image, sums = call(
        image_kernel,
        geometry_specs + [VMEM] * 4,
        [array(1024), array(1024), array(slabs * sectors)],
        [pltpu.VMEM((128, 128), F32), pltpu.VMEM((256, 128), F32)],
        "image",
    )(*geometry, part, normals, below, above)
    sums = lax.all_to_all(
        sums.reshape(slabs * sectors, 1, 128),
        ("stream", "azim"),
        split_axis=0,
        concat_axis=0,
        tiled=True,
    ).reshape(slabs * sectors, 128)
    velocity, pressure = call(
        final_kernel,
        geometry_specs + [VMEM] * 4,
        [array(3 * 1024), array(1024)],
        [],
        "velocity",
    )(*geometry, sums, field, image, pred)
    return velocity.reshape(3, 4, 4, 4, 4, 4, 128), pressure.reshape(4, 4, 4, 4, 4, 128)


def solution(mesh):
    in_specs = (
        P(None, None, None, ("stream", "azim")),
        P(("stream", "azim")),
        P(),
        P(),
        P(),
        P("stream", "azim", None),
    )
    out_specs = (
        P(None, None, None, None, "stream", "azim", None),
        P(None, None, None, "stream", "azim", None),
    )
    return jax.shard_map(body, mesh=mesh, in_specs=in_specs, out_specs=out_specs, check_vma=False)
```

```python
import functools
import math

import jax
import jax.numpy as jnp
import numpy as np
from jax import lax
from jax.experimental import pallas as pl
from jax.experimental.pallas import tpu as pltpu
from jax.sharding import PartitionSpec as P

CAP = 2
DT = 0.01
PENALTY = 100.0
VMEM_LIMIT = 40 * 1024 * 1024
PACK_LIMIT = 60 * 1024 * 1024
F32 = jnp.float32


def node_tables():
    root = 1.0 / math.sqrt(5.0)
    points = np.array([-1.0, -root, root, 1.0])
    weights = np.array([1.0 / 6.0, 5.0 / 6.0, 5.0 / 6.0, 1.0 / 6.0])
    legendre = (5.0 * points**3 - 3.0 * points) / 2.0
    slope = np.zeros((4, 4))
    for first in range(4):
        for second in range(4):
            if first != second:
                slope[first, second] = legendre[first] / (
                    legendre[second] * (points[first] - points[second])
                )
    slope[0, 0] = -3.0
    slope[3, 3] = 3.0
    return slope, weights


SLOPE, WEIGHT = node_tables()
STIFF = SLOPE.T @ np.diag(WEIGHT) @ SLOPE
EDGE = float(WEIGHT[0])

ROWS = 8
BLOCK_ROWS = 24
PEER_ROWS = CAP * BLOCK_ROWS + ROWS


def iotas():
    lane = lax.broadcasted_iota(jnp.int32, (ROWS, 128), 1)
    sub = lax.broadcasted_iota(jnp.int32, (ROWS, 128), 0)
    return lane, sub


def lanes(x, shift):
    shift %= 128
    return pltpu.roll(x, shift, 1) if shift else x


def subs(x, shift):
    shift %= ROWS
    return pltpu.roll(x, shift, 0) if shift else x


def combine(coefs, values, factor=1.0):
    total = None
    for coef, value in zip(coefs, values):
        coef = factor * float(coef)
        term = coef * value
        total = term if total is None else total + term
    return total


def halves(line):
    return (line[0] + line[3], line[1] + line[2]), (line[0] - line[3], line[1] - line[2])


def slope_along(line):
    even, odd = halves(line)
    first = [combine(SLOPE[i, :2] - SLOPE[i, :1:-1], odd, 0.5) for i in range(2)]
    second = [combine(SLOPE[i, :2] + SLOPE[i, :1:-1], even, 0.5) for i in range(2)]
    return [first[0] + second[0], first[1] + second[1], first[1] - second[1], first[0] - second[0]]


def stiff_along(line):
    even, odd = halves(line)
    first = [combine(STIFF[i, :2] + STIFF[i, :1:-1], even, 0.5) for i in range(2)]
    second = [combine(STIFF[i, :2] - STIFF[i, :1:-1], odd, 0.5) for i in range(2)]
    return [first[0] + second[0], first[1] + second[1], first[1] - second[1], first[0] - second[0]]


def choose(key, values):
    result = values[0]
    for at in range(1, len(values)):
        result = jnp.where(key == at, values[at], result)
    return result


def swap_groups(tiles, group):
    mixed = [lanes(tile, 16 * t) for t, tile in enumerate(tiles)]
    for bit in (1, 2, 4):
        odd = (group & bit) != 0
        mixed = [jnp.where(odd, mixed[(t + bit) & 7], mixed[t]) for t in range(8)]
    return [lanes(mixed[-g & 7], -16 * g) for g in range(8)]


CHUNKS = 4


def pack_kernel(
    ids_h, axial_h, azim_h, radial_h, hist_h, send_h, keep_h,
    hist, send, keep, ids, len_axial, len_azim, len_radial, count, labels, table,
    hist_sem, keep_sem, small_sem,
):
    sectors = lax.axis_size("azim")
    peers = lax.axis_size("stream")
    me = lax.axis_index("stream")
    width = hist.shape[1] // CHUNKS
    columns = width // 128

    def chunk(n):
        span = pl.ds(pl.multiple_of(n * width, width), width)
        return pltpu.make_async_copy(hist_h.at[:, span], hist.at[:, span], hist_sem.at[n])

    def kept(n):
        rows = keep.shape[0] // CHUNKS
        span = pl.ds(pl.multiple_of(n * rows, rows), rows)
        return pltpu.make_async_copy(keep.at[span, :], keep_h.at[span, :], keep_sem.at[n])

    small = [
        pltpu.make_async_copy(source, target, small_sem.at[n])
        for n, (source, target) in enumerate(
            ((ids_h, ids), (axial_h, len_axial), (azim_h, len_azim), (radial_h, len_radial))
        )
    ]
    for copy in small:
        copy.start()
    for n in range(CHUNKS):
        chunk(n).start()
    lane, sub = iotas()
    group = lane >> 4
    c_at = sub & 3
    for t in range(peers):
        count[t] = 0
    for n in range(CAP * peers):
        labels[n] = 0
    for copy in small:
        copy.wait()
    whole = jnp.broadcast_to(len_radial[...], (ROWS, 128))
    rows = choose(sub, [lanes(whole, -16 * z) for z in range(8)])
    rows = jnp.where(group == 0, rows, 0.0)
    for shift in (16, 32, 64):
        rows = rows + lanes(rows, shift)
    table[...] = rows

    def pattern(low, high):
        return jnp.where(sub < 4, F32(low), F32(high))

    def column(at):
        offset = pl.multiple_of(at * 128, 128)

        def level(which, comp, t):
            return hist[pl.ds((which * 3 + comp) * 64 + 8 * t, ROWS), pl.ds(offset, 128)]

        places = []
        axial = azim = radial = None
        for piece in range(8):
            ident = ids[at * 8 + piece]
            owner = ident >> 7
            slot = ident & 127
            flow = owner // sectors
            sector = owner - flow * sectors
            moving = flow != me
            rank = jnp.where(moving, count[flow], 0)
            count[flow] = rank + 1
            labels[jnp.where(moving, flow * CAP + rank, CAP * peers)] = slot + 1
            places.append(
                (flow * PEER_ROWS + rank * BLOCK_ROWS, (at * 8 + piece) * BLOCK_ROWS)
            )
            one_axial = len_axial[flow * 4 + (slot >> 5)]
            one_azim = len_azim[sector * 4 + ((slot >> 3) & 3)]
            one_radial = table[pl.ds(slot & 7, 1), :]
            if piece == 0:
                axial = jnp.full((ROWS, 128), one_axial, F32)
                azim = jnp.full((ROWS, 128), one_azim, F32)
                radial = jnp.broadcast_to(one_radial, (ROWS, 128))
            else:
                axial = jnp.where(group == piece, one_axial, axial)
                azim = jnp.where(group == piece, one_azim, azim)
                radial = jnp.where(group == piece, one_radial, radial)
        scales = [(-2.0 * DT) / length for length in (axial, azim, radial)]

        extrap = [
            [3.0 * (level(0, comp, t) - level(1, comp, t)) + level(2, comp, t) for t in range(8)]
            for comp in range(3)
        ]
        wind = [[scales[axis] * extrap[axis][t] for t in range(8)] for axis in range(3)]
        spin = []
        for k in range(4):
            value = jnp.zeros((ROWS, 128), F32)
            for c in range(4):
                value = jnp.where(c_at == c, F32(SLOPE[c, (c + k) % 4]), value)
            spin.append(value)
        same = [[pattern(SLOPE[2 * p, 2 * o], SLOPE[2 * p + 1, 2 * o + 1]) for o in range(2)] for p in range(2)]
        cross = [[pattern(SLOPE[2 * p, 2 * o + 1], SLOPE[2 * p + 1, 2 * o]) for o in range(2)] for p in range(2)]
        for comp in range(3):
            ue = extrap[comp]
            flipped = [subs(ue[t], 4) for t in range(8)]
            along_a = [None] * 8
            for half in range(2):
                for a, value in enumerate(slope_along([ue[2 * o + half] for o in range(4)])):
                    along_a[2 * a + half] = value
            tiles = []
            for t in range(8):
                a, half = t // 2, t % 2
                along_b = (
                    same[half][0] * ue[2 * a]
                    + cross[half][0] * flipped[2 * a]
                    + same[half][1] * ue[2 * a + 1]
                    + cross[half][1] * flipped[2 * a + 1]
                )
                along_c = spin[0] * ue[t]
                for k in range(1, 4):
                    along_c = along_c + spin[k] * subs(jnp.where(c_at < k, flipped[t], ue[t]), -k)
                advect = wind[0][t] * along_a[t] + wind[1][t] * along_b + wind[2][t] * along_c
                base = ue[t] + 1.5 * level(1, comp, t) - F32(2.0 / 3.0) * level(2, comp, t)
                tiles.append(base + advect)
            for (to_send, to_keep), tile in zip(places, swap_groups(tiles, group)):
                send[pl.ds(pl.multiple_of(to_send + comp * ROWS, ROWS), ROWS), :] = tile
                keep[pl.ds(pl.multiple_of(to_keep + comp * ROWS, ROWS), ROWS), :] = tile

    @pl.loop(0, CHUNKS)
    def _(n):
        chunk(n).wait()
        for k in range(columns):
            column(n * columns + k)
        kept(n).start()

    corner = sub == 0
    for t in range(peers):
        marks = jnp.zeros((ROWS, 128), jnp.int32)
        for rank in range(CAP):
            marks = jnp.where(corner & (lane == CAP * me + rank), labels[t * CAP + rank], marks)
        send[pl.ds(t * PEER_ROWS + CAP * BLOCK_ROWS, ROWS), :] = marks.astype(F32)
    leaving = pltpu.make_async_copy(send, send_h, small_sem.at[0])
    leaving.start()
    for n in range(CHUNKS):
        kept(n).wait()
    leaving.wait()


def at(a, b, c, h):
    return pl.ds((a * 16 + b * 4 + c) * 16 + h * ROWS, ROWS)


def join_radial(line, lane):
    first = line[0] + jnp.where(lane == 0, 0.0, lanes(line[3], 1))
    last = jnp.where(lane == 127, 0.0, lanes(first, -1))
    return [first, line[1], line[2], last]


def join_azim(ref, sub):
    ey = sub & 3
    for a in range(4):
        for c in range(4):
            for h in range(2):
                low = ref[at(a, 0, c, h), :]
                high = ref[at(a, 3, c, h), :]
                ref[at(a, 0, c, h), :] = low + jnp.where(ey == 0, 0.0, subs(high, 1))
                ref[at(a, 3, c, h), :] = high + jnp.where(ey == 3, 0.0, subs(low, -1))


def join_axial(ref, b, c, sub):
    top = sub < 4
    low = [ref[at(0, b, c, h), :] for h in range(2)]
    high = [ref[at(3, b, c, h), :] for h in range(2)]
    low_turned = [subs(x, 4) for x in low]
    high_turned = [subs(x, 4) for x in high]
    new_low = [
        low[0] + jnp.where(top, 0.0, high_turned[0]),
        low[1] + jnp.where(top, high_turned[0], high_turned[1]),
    ]
    new_high = [
        high[0] + jnp.where(top, low_turned[0], low_turned[1]),
        high[1] + jnp.where(top, low_turned[1], 0.0),
    ]
    return new_low, new_high


def lengths(len_axial, len_azim, len_radial, sub):
    slab = lax.axis_index("stream")
    sector = lax.axis_index("azim")
    columns, rows = len_axial.shape[0], len_azim.shape[0]
    x0, y0 = slab * 4, sector * 4
    top = sub < 4
    axial = [jnp.where(top, len_axial[x0 + 2 * h], len_axial[x0 + 2 * h + 1]) for h in range(2)]
    azim = choose(sub & 3, [jnp.full((ROWS, 128), len_azim[y0 + k], F32) for k in range(4)])
    radial = jnp.broadcast_to(len_radial[...], (ROWS, 128))
    before = len_axial[jnp.maximum(x0 - 1, 0)]
    after = len_axial[jnp.minimum(x0 + 4, columns - 1)]
    below = len_azim[lax.rem(y0 + rows - 1, rows)]
    above = len_azim[lax.rem(y0 + 4, rows)]
    return axial, azim, radial, (before, after, below, above)


def load_kernel(
    ids, len_axial, len_azim, len_radial, solid, arrived, keep, pred, part, up, down,
    marks, marks_s, source, sem,
):
    lane, sub = iotas()
    group = lane >> 4
    peers = arrived.shape[0] // PEER_ROWS
    total = None
    for t in range(peers):
        tile = arrived[pl.ds(t * PEER_ROWS + CAP * BLOCK_ROWS, ROWS), :]
        total = tile if total is None else total + tile
    marks[...] = total.astype(jnp.int32)
    scalars = pltpu.make_async_copy(marks, marks_s, sem)
    scalars.start()
    slab, sectors = lax.axis_index("stream"), lax.axis_size("azim")
    for p in range(ids.shape[0]):
        ident = ids[p]
        stays = (ident >> 7) // sectors == slab
        source[jnp.where(stays, ident & 127, 128)] = -1 - p * BLOCK_ROWS
    scalars.wait()
    for n in range(peers * CAP):
        label = marks_s[0, n]
        source[jnp.where(label > 0, label - 1, 128)] = (
            (n // CAP) * PEER_ROWS + (n % CAP) * BLOCK_ROWS
        )

    def unpack(j, carry):
        places = [source[j * 8 + g] for g in range(8)]
        for comp in range(3):
            tiles = []
            for g, place in enumerate(places):
                row = pl.multiple_of(jnp.maximum(-1 - place, 0) + comp * ROWS, ROWS)
                kept = keep[pl.ds(row, ROWS), :]
                row = pl.multiple_of(jnp.maximum(place, 0) + comp * ROWS, ROWS)
                tiles.append(jnp.where(place >= 0, arrived[pl.ds(row, ROWS), :], kept))
            for t, tile in enumerate(swap_groups(tiles, group)):
                pred[pl.ds(comp * 1024 + 8 * t * 16 + j, ROWS, stride=16), :] = tile
        return carry

    lax.fori_loop(0, 16, unpack, 0, unroll=4)

    axial, azim, radial, _ = lengths(len_axial, len_azim, len_radial, sub)
    inverse = [
        1.0 / (F32(11.0 / 6.0) + F32(DT * PENALTY) * solid[pl.ds(h * ROWS, ROWS), :].astype(F32))
        for h in range(2)
    ]

    def scaled(comp, a, b, c, h):
        spot = pl.ds(comp * 1024 + (a * 16 + b * 4 + c) * 16 + h * ROWS, ROWS)
        value = pred[spot, :] * inverse[h]
        pred[spot, :] = value
        return value

    area = [
        [0.25 * azim * radial for h in range(2)],
        [0.25 * axial[h] * radial for h in range(2)],
        [0.25 * axial[h] * azim for h in range(2)],
    ]
    for h in range(2):
        for b in range(4):
            for c in range(4):
                line = [scaled(0, a, b, c, h) for a in range(4)]
                for a, value in enumerate(slope_along(line)):
                    part[at(a, b, c, h), :] = area[0][h] * value
        for a in range(4):
            for c in range(4):
                line = [scaled(1, a, b, c, h) for b in range(4)]
                for b, value in enumerate(slope_along(line)):
                    part[at(a, b, c, h), :] += area[1][h] * value
        for a in range(4):
            for b in range(4):
                line = [scaled(2, a, b, c, h) for c in range(4)]
                line = [
                    float(-WEIGHT[a] * WEIGHT[b] * WEIGHT[c])
                    * (part[at(a, b, c, h), :] + area[2][h] * value)
                    for c, value in enumerate(slope_along(line))
                ]
                for c, value in enumerate(join_radial(line, lane)):
                    part[at(a, b, c, h), :] = value
    join_azim(part, sub)
    top = sub < 4
    for b in range(4):
        for c in range(4):
            low, high = join_axial(part, b, c, sub)
            for h in range(2):
                part[at(0, b, c, h), :] = low[h]
                part[at(3, b, c, h), :] = high[h]
            inner = [[part[at(a, b, c, h), :] for a in (1, 2)] for h in range(2)]
            spot = pl.ds((b * 4 + c) * ROWS, ROWS)
            normal = combine(STIFF[3], [low[1], *inner[1], high[1]])
            up[spot, :] = jnp.where(top, subs(high[1], 4), normal)
            normal = combine(STIFF[0], [low[0], *inner[0], high[0]])
            down[spot, :] = jnp.where(top, low[0], subs(normal, 4))


def axial_kernel(part, below, above, field, normals, up, down):
    lane, sub = iotas()
    top = sub < 4
    slab = lax.axis_index("stream")
    first = jnp.where(slab == 0, F32(0.0), F32(1.0))
    last = jnp.where(slab == lax.axis_size("stream") - 1, F32(0.0), F32(1.0))
    for b in range(4):
        for c in range(4):
            spot = pl.ds((b * 4 + c) * ROWS, ROWS)
            low = part[at(0, b, c, 0), :]
            high = part[at(3, b, c, 1), :]
            under, over = below[spot, :], above[spot, :]
            normals[spot, :] = jnp.where(
                top,
                subs(under, 4) + float(STIFF[3, 3]) * low,
                over + float(STIFF[0, 0]) * high,
            )
            field[at(0, b, c, 0), :] = low + jnp.where(top, first * under, 0.0)
            field[at(3, b, c, 1), :] = jnp.where(top, high, last * (high + subs(over, 4)))
            field[at(0, b, c, 1), :] = part[at(0, b, c, 1), :]
            field[at(3, b, c, 0), :] = part[at(3, b, c, 0), :]
            for a in (1, 2):
                for h in range(2):
                    field[at(a, b, c, h), :] = part[at(a, b, c, h), :]
    ey = sub & 3
    for a in range(4):
        for c in range(4):
            spot = pl.ds((a * 4 + c) * ROWS, ROWS)
            line = [[field[at(a, b, c, h), :] for b in range(4)] for h in range(2)]
            normal = [combine(STIFF[3], line[h]) for h in range(2)]
            up[spot, :] = choose(
                ey, [subs(normal[1], -3), subs(normal[0], -2), subs(line[1][3], -1), line[0][3]]
            )
            normal = [combine(STIFF[0], line[h]) for h in range(2)]
            down[spot, :] = choose(
                ey, [line[0][0], subs(line[1][0], 1), subs(normal[0], 2), subs(normal[1], 3)]
            )
    spot = pl.ds(16 * ROWS, ROWS)
    edge = [normals[pl.ds((12 + c) * ROWS, ROWS), :] for c in range(4)]
    up[spot, :] = choose(ey, [subs(edge[3], -3), subs(edge[2], -2), subs(edge[1], -1), edge[0]])
    edge = [normals[pl.ds(c * ROWS, ROWS), :] for c in range(4)]
    down[spot, :] = choose(ey, [edge[0], subs(edge[1], 1), subs(edge[2], 2), subs(edge[3], 3)])


def image_kernel(
    len_axial, len_azim, len_radial, part, normals_in, below, above, field, image, sums, normals, sides
):
    lane, sub = iotas()
    top = sub < 4
    ey = sub & 3
    slab = lax.axis_index("stream")
    first = jnp.where(slab == 0, F32(0.0), F32(1.0))
    last = jnp.where(slab == lax.axis_size("stream") - 1, F32(0.0), F32(1.0))
    for a in range(4):
        for c in range(4):
            spot = pl.ds((a * 4 + c) * ROWS, ROWS)
            under, over = below[spot, :], above[spot, :]
            under_face = [subs(under, -3), subs(under, -2)]
            under_normal = [subs(under, -1), under]
            over_face = [subs(over, 3), subs(over, 2)]
            over_normal = [subs(over, 1), over]
            for h in range(2):
                low = part[at(a, 0, c, h), :]
                high = part[at(a, 3, c, h), :]
                sides[pl.ds(((a * 4 + c) * 2 + h) * ROWS, ROWS), :] = jnp.where(
                    ey == 0,
                    under_normal[h] + float(STIFF[3, 3]) * low,
                    over_normal[h] + float(STIFF[0, 0]) * high,
                )
                field[at(a, 0, c, h), :] = low + jnp.where(ey == 0, under_face[h], 0.0)
                field[at(a, 3, c, h), :] = high + jnp.where(ey == 3, over_face[h], 0.0)
                for b in (1, 2):
                    field[at(a, b, c, h), :] = part[at(a, b, c, h), :]
    under, over = below[pl.ds(16 * ROWS, ROWS), :], above[pl.ds(16 * ROWS, ROWS), :]
    for c in range(4):
        spot = pl.ds(c * ROWS, ROWS)
        normals[spot, :] = normals_in[spot, :] + jnp.where(ey == 0, subs(under, c - 3), 0.0)
        spot = pl.ds((12 + c) * ROWS, ROWS)
        normals[spot, :] = normals_in[spot, :] + jnp.where(ey == 3, subs(over, 3 - c), 0.0)
        for b in (1, 2):
            spot = pl.ds((b * 4 + c) * ROWS, ROWS)
            normals[spot, :] = normals_in[spot, :]

    axial, azim, radial, (before, after, beneath, beyond) = lengths(
        len_axial, len_azim, len_radial, sub
    )
    zero = jnp.zeros((ROWS, 128), F32)
    rx = [2.0 / axial[h] for h in range(2)]
    ry = 2.0 / azim
    rz = 2.0 / radial
    qz = 0.5 * radial
    qx = [[0.5 * axial[h] for a in range(4)] for h in range(2)]
    before_v, after_v = jnp.full((ROWS, 128), before, F32), jnp.full((ROWS, 128), after, F32)
    beneath_v, beyond_v = jnp.full((ROWS, 128), beneath, F32), jnp.full((ROWS, 128), beyond, F32)
    own_x = [qx[h][0] for h in range(2)]
    qx[0][0] = own_x[0] + jnp.where(top, first * 0.5 * before_v, 0.0)
    qx[1][3] = own_x[1] + jnp.where(top, 0.0, last * 0.5 * after_v)
    ghost_x = [jnp.where(top, first * 2.0 / before_v, 0.0), jnp.where(top, 0.0, last * 2.0 / after_v)]
    own_y = 0.5 * azim
    qy = [
        own_y + jnp.where(ey == 0, 0.5 * beneath_v, 0.0),
        own_y,
        own_y,
        own_y + jnp.where(ey == 3, 0.5 * beyond_v, 0.0),
    ]
    ghost_y = [jnp.where(ey == 0, 2.0 / beneath_v, 0.0), zero, zero, jnp.where(ey == 3, 2.0 / beyond_v, 0.0)]

    for h in range(2):
        factor = [rx[h] * qz * qy[b] for b in range(4)]
        extra = [ghost_x[h] * qz * qy[b] for b in range(4)]
        edge_a = 0 if h == 0 else 3
        for b in range(4):
            for c in range(4):
                line = [field[at(a, b, c, h), :] for a in range(4)]
                for a, value in enumerate(stiff_along(line)):
                    value = factor[b] * value
                    if a == edge_a:
                        value = value + extra[b] * normals[pl.ds((b * 4 + c) * ROWS, ROWS), :]
                    image[at(a, b, c, h), :] = float(WEIGHT[b] * WEIGHT[c]) * value
        for a in range(4):
            factor_a = ry * qz * qx[h][a]
            extra_a = [ghost_y[b] * qz * qx[h][a] for b in range(4)]
            for c in range(4):
                line = [field[at(a, b, c, h), :] for b in range(4)]
                side = sides[pl.ds(((a * 4 + c) * 2 + h) * ROWS, ROWS), :]
                for b, value in enumerate(stiff_along(line)):
                    value = factor_a * value
                    if b in (0, 3):
                        value = value + extra_a[b] * side
                    image[at(a, b, c, h), :] += float(WEIGHT[a] * WEIGHT[c]) * value
        for a in range(4):
            for b in range(4):
                factor_ab = (float(WEIGHT[a] * WEIGHT[b]) * rz) * qx[h][a] * qy[b]
                line = [field[at(a, b, c, h), :] for c in range(4)]
                line = [
                    image[at(a, b, c, h), :] + factor_ab * value
                    for c, value in enumerate(stiff_along(line))
                ]
                for c, value in enumerate(join_radial(line, lane)):
                    image[at(a, b, c, h), :] = value
    join_azim(image, sub)
    outlet = jnp.where(top, 1.0, last)
    for b in range(4):
        for c in range(4):
            low, high = join_axial(image, b, c, sub)
            high[1] = high[1] * outlet
            for h in range(2):
                image[at(0, b, c, h), :] = low[h]
                image[at(3, b, c, h), :] = high[h]

    load_load = load_image = image_image = zero
    for h in range(2):
        for a in range(3):
            for b in range(3):
                for c in range(3):
                    one, two = field[at(a, b, c, h), :], image[at(a, b, c, h), :]
                    load_load = load_load + one * one
                    load_image = load_image + one * two
                    image_image = image_image + two * two
    energy = zero
    for h in range(2):
        along = [zero, zero, zero]
        for m in range(4):
            for n in range(4):
                weight = float(WEIGHT[m] * WEIGHT[n])
                lines = (
                    [image[at(k, m, n, h), :] for k in range(4)],
                    [image[at(m, k, n, h), :] for k in range(4)],
                    [image[at(m, n, k, h), :] for k in range(4)],
                )
                for axis, line in enumerate(lines):
                    dot = None
                    for one, two in zip(line, stiff_along(line)):
                        term = one * two
                        dot = term if dot is None else dot + term
                    along[axis] = along[axis] + weight * dot
        energy = (
            energy
            + rx[h] * own_y * qz * along[0]
            + ry * own_x[h] * qz * along[1]
            + rz * own_x[h] * own_y * along[2]
        )
    row = zero
    for k, value in enumerate((load_load, load_image, image_image, energy)):
        value = jnp.sum(jnp.sum(value, axis=0, keepdims=True), axis=1, keepdims=True)
        row = jnp.where(lane == k, jnp.broadcast_to(value, (ROWS, 128)), row)
    for k in range(sums.shape[0] // ROWS):
        sums[pl.ds(k * ROWS, ROWS), :] = row


def final_kernel(
    len_axial, len_azim, len_radial, sums, field, image, pred, velocity_h, pressure_h, velocity, pressure, sems
):
    lane, sub = iotas()
    total = sums[pl.ds(0, ROWS), :]
    for k in range(1, sums.shape[0] // ROWS):
        total = total + sums[pl.ds(k * ROWS, ROWS), :]
    total = jnp.broadcast_to(jnp.sum(total, axis=0, keepdims=True), (ROWS, 128))
    s0, s1, s2, s3 = (
        jnp.broadcast_to(
            jnp.sum(jnp.where(lane == k, total, 0.0), axis=1, keepdims=True), (ROWS, 128)
        )
        for k in range(4)
    )
    alpha = s0 / s1
    ratio = s2 / s1
    grown = alpha * ratio
    energy = alpha * (s3 - s2 * ratio)
    second = s0 * (grown - 1.0) / (alpha * energy)
    of_load = alpha + second * grown
    of_image = -(second * alpha)

    axial, azim, radial, _ = lengths(len_axial, len_azim, len_radial, sub)
    for h in range(2):
        for a in range(4):
            for b in range(4):
                for c in range(4):
                    spot = at(a, b, c, h)
                    pressure[spot, :] = of_load * field[spot, :] + of_image * image[spot, :]
    leaving = [pltpu.make_async_copy(pressure, pressure_h, sems.at[3])]
    leaving[0].start()
    for axis in range(3):
        for h in range(2):
            scale = 2.0 / (axial[h], azim, radial)[axis]
            for m in range(4):
                for n in range(4):
                    line = [(k, m, n) if axis == 0 else (m, k, n) if axis == 1 else (m, n, k) for k in range(4)]
                    values = slope_along([pressure[at(*node, h), :] for node in line])
                    for (a, b, c), value in zip(line, values):
                        spot = pl.ds(axis * 1024 + (a * 16 + b * 4 + c) * 16 + h * ROWS, ROWS)
                        velocity[spot, :] = pred[spot, :] - scale * value
        span = pl.ds(axis * 1024, 1024)
        leaving.append(pltpu.make_async_copy(velocity.at[span, :], velocity_h.at[span, :], sems.at[axis]))
        leaving[-1].start()
    for copy in leaving:
        copy.wait()


SMEM = pl.BlockSpec(memory_space=pltpu.SMEM)
VMEM = pl.BlockSpec(memory_space=pltpu.VMEM)
HBM = pl.BlockSpec(memory_space=pltpu.HBM)


def array(rows, kind=F32):
    return jax.ShapeDtypeStruct((rows, 128), kind)


def call(kernel, ins, outs, scratch, name, place=VMEM, limit=VMEM_LIMIT):
    return pl.pallas_call(
        kernel,
        out_shape=outs,
        in_specs=ins,
        out_specs=[place] * len(outs),
        scratch_shapes=scratch,
        compiler_params=pltpu.CompilerParams(vmem_limit_bytes=limit),
        name=name,
    )


def shifted(axis, value, shift):
    count = lax.axis_size(axis)
    return lax.ppermute(value, axis, [(i, (i + shift) % count) for i in range(count)])


def body(history, block_ids, len_axial, len_azim, len_radial, solid):
    slabs, sectors = lax.axis_size("stream"), lax.axis_size("azim")
    radial = len_radial.reshape(1, 128)
    geometry = (len_axial, len_azim, radial)
    geometry_specs = [SMEM, SMEM, VMEM]
    hist = history.reshape(576, history.shape[3])
    send, keep = call(
        pack_kernel,
        [HBM] * 5,
        [array(slabs * PEER_ROWS), array(128 * BLOCK_ROWS)],
        [
            pltpu.VMEM(hist.shape, F32),
            pltpu.VMEM((slabs * PEER_ROWS, 128), F32),
            pltpu.VMEM((128 * BLOCK_ROWS, 128), F32),
            pltpu.SMEM(block_ids.shape, jnp.int32),
            pltpu.SMEM(len_axial.shape, F32),
            pltpu.SMEM(len_azim.shape, F32),
            pltpu.VMEM((1, 128), F32),
            pltpu.SMEM((slabs,), jnp.int32),
            pltpu.SMEM((CAP * slabs + 1,), jnp.int32),
            pltpu.VMEM((ROWS, 128), F32),
            pltpu.SemaphoreType.DMA((CHUNKS,)),
            pltpu.SemaphoreType.DMA((CHUNKS,)),
            pltpu.SemaphoreType.DMA((4,)),
        ],
        "pack",
        HBM,
        limit=PACK_LIMIT,
    )(block_ids, *geometry, hist)
    arrived = lax.all_to_all(
        send.reshape(slabs, PEER_ROWS, 128), "stream", split_axis=0, concat_axis=0, tiled=True
    ).reshape(slabs * PEER_ROWS, 128)
    pred, part, up, down = call(
        load_kernel,
        [SMEM] + geometry_specs + [VMEM] * 3,
        [array(3 * 1024), array(1024), array(128), array(128)],
        [
            pltpu.VMEM((ROWS, 128), jnp.int32),
            pltpu.SMEM((ROWS, 128), jnp.int32),
            pltpu.SMEM((129,), jnp.int32),
            pltpu.SemaphoreType.DMA(()),
        ],
        "load",
    )(block_ids, *geometry, solid.reshape(16, 128), arrived, keep)
    below, above = shifted("stream", up, 1), shifted("stream", down, -1)
    part, normals, up, down = call(
        axial_kernel,
        [VMEM] * 3,
        [array(1024), array(128), array(136), array(136)],
        [],
        "axial_faces",
    )(part, below, above)
    below, above = shifted("azim", up, 1), shifted("azim", down, -1)
    field, image, sums = call(
        image_kernel,
        geometry_specs + [VMEM] * 4,
        [array(1024), array(1024), array(slabs * sectors)],
        [pltpu.VMEM((128, 128), F32), pltpu.VMEM((256, 128), F32)],
        "image",
    )(*geometry, part, normals, below, above)
    sums = lax.all_to_all(
        sums.reshape(slabs * sectors, 1, 128),
        ("stream", "azim"),
        split_axis=0,
        concat_axis=0,
        tiled=True,
    ).reshape(slabs * sectors, 128)
    velocity, pressure = call(
        final_kernel,
        geometry_specs + [VMEM] * 4,
        [array(3 * 1024), array(1024)],
        [
            pltpu.VMEM((3 * 1024, 128), F32),
            pltpu.VMEM((1024, 128), F32),
            pltpu.SemaphoreType.DMA((4,)),
        ],
        "velocity",
        HBM,
    )(*geometry, sums, field, image, pred)
    return velocity.reshape(3, 4, 4, 4, 4, 4, 128), pressure.reshape(4, 4, 4, 4, 4, 128)


def solution(mesh):
    in_specs = (
        P(None, None, None, ("stream", "azim")),
        P(("stream", "azim")),
        P(),
        P(),
        P(),
        P("stream", "azim", None),
    )
    out_specs = (
        P(None, None, None, None, "stream", "azim", None),
        P(None, None, None, "stream", "azim", None),
    )
    return jax.shard_map(body, mesh=mesh, in_specs=in_specs, out_specs=out_specs, check_vma=False)
```

```python
import functools
import math

import jax
import jax.numpy as jnp
import numpy as np
from jax import lax
from jax.experimental import pallas as pl
from jax.experimental.pallas import tpu as pltpu
from jax.sharding import PartitionSpec as P

CAP = 2
DT = 0.01
PENALTY = 100.0
VMEM_LIMIT = 40 * 1024 * 1024
PACK_LIMIT = 60 * 1024 * 1024
F32 = jnp.float32


def node_tables():
    root = 1.0 / math.sqrt(5.0)
    points = np.array([-1.0, -root, root, 1.0])
    weights = np.array([1.0 / 6.0, 5.0 / 6.0, 5.0 / 6.0, 1.0 / 6.0])
    legendre = (5.0 * points**3 - 3.0 * points) / 2.0
    slope = np.zeros((4, 4))
    for first in range(4):
        for second in range(4):
            if first != second:
                slope[first, second] = legendre[first] / (
                    legendre[second] * (points[first] - points[second])
                )
    slope[0, 0] = -3.0
    slope[3, 3] = 3.0
    return slope, weights


SLOPE, WEIGHT = node_tables()
STIFF = SLOPE.T @ np.diag(WEIGHT) @ SLOPE
EDGE = float(WEIGHT[0])

ROWS = 8
BLOCK_ROWS = 24
PEER_ROWS = CAP * BLOCK_ROWS + ROWS


def iotas():
    lane = lax.broadcasted_iota(jnp.int32, (ROWS, 128), 1)
    sub = lax.broadcasted_iota(jnp.int32, (ROWS, 128), 0)
    return lane, sub


def lanes(x, shift):
    shift %= 128
    return pltpu.roll(x, shift, 1) if shift else x


def subs(x, shift):
    shift %= ROWS
    return pltpu.roll(x, shift, 0) if shift else x


def combine(coefs, values, factor=1.0):
    total = None
    for coef, value in zip(coefs, values):
        coef = factor * float(coef)
        term = coef * value
        total = term if total is None else total + term
    return total


def halves(line):
    return (line[0] + line[3], line[1] + line[2]), (line[0] - line[3], line[1] - line[2])


def slope_along(line):
    even, odd = halves(line)
    first = [combine(SLOPE[i, :2] - SLOPE[i, :1:-1], odd, 0.5) for i in range(2)]
    second = [combine(SLOPE[i, :2] + SLOPE[i, :1:-1], even, 0.5) for i in range(2)]
    return [first[0] + second[0], first[1] + second[1], first[1] - second[1], first[0] - second[0]]


def stiff_along(line):
    even, odd = halves(line)
    first = [combine(STIFF[i, :2] + STIFF[i, :1:-1], even, 0.5) for i in range(2)]
    second = [combine(STIFF[i, :2] - STIFF[i, :1:-1], odd, 0.5) for i in range(2)]
    return [first[0] + second[0], first[1] + second[1], first[1] - second[1], first[0] - second[0]]


def choose(key, values):
    result = values[0]
    for at in range(1, len(values)):
        result = jnp.where(key == at, values[at], result)
    return result


def swap_groups(tiles, group):
    mixed = [lanes(tile, 16 * t) for t, tile in enumerate(tiles)]
    for bit in (1, 2, 4):
        odd = (group & bit) != 0
        mixed = [jnp.where(odd, mixed[(t + bit) & 7], mixed[t]) for t in range(8)]
    return [lanes(mixed[-g & 7], -16 * g) for g in range(8)]


CHUNKS = 4


def pack_kernel(
    ids_h, axial_h, azim_h, radial_h, hist_h, send_h, keep_h,
    hist, send, keep, ids, len_axial, len_azim, len_radial, count, labels, table,
    hist_sem, keep_sem, small_sem,
):
    sectors = lax.axis_size("azim")
    peers = lax.axis_size("stream")
    me = lax.axis_index("stream")
    width = hist.shape[1] // CHUNKS
    columns = width // 128

    def chunk(n):
        span = pl.ds(pl.multiple_of(n * width, width), width)
        return pltpu.make_async_copy(hist_h.at[:, span], hist.at[:, span], hist_sem.at[n])

    def kept(n):
        rows = keep.shape[0] // CHUNKS
        span = pl.ds(pl.multiple_of(n * rows, rows), rows)
        return pltpu.make_async_copy(keep.at[span, :], keep_h.at[span, :], keep_sem.at[n])

    small = [
        pltpu.make_async_copy(source, target, small_sem.at[n])
        for n, (source, target) in enumerate(
            ((ids_h, ids), (axial_h, len_axial), (azim_h, len_azim), (radial_h, len_radial))
        )
    ]
    for copy in small:
        copy.start()
    for n in range(CHUNKS):
        chunk(n).start()
    lane, sub = iotas()
    group = lane >> 4
    c_at = sub & 3
    for t in range(peers):
        count[t] = 0
    for n in range(CAP * peers):
        labels[n] = 0
    for copy in small:
        copy.wait()
    whole = jnp.broadcast_to(len_radial[...], (ROWS, 128))
    rows = choose(sub, [lanes(whole, -16 * z) for z in range(8)])
    rows = jnp.where(group == 0, rows, 0.0)
    for shift in (16, 32, 64):
        rows = rows + lanes(rows, shift)
    table[...] = rows

    def pattern(low, high):
        return jnp.where(sub < 4, F32(low), F32(high))

    def column(at):
        offset = pl.multiple_of(at * 128, 128)

        def level(which, comp, t):
            return hist[pl.ds((which * 3 + comp) * 64 + 8 * t, ROWS), pl.ds(offset, 128)]

        places = []
        axial = azim = radial = None
        for piece in range(8):
            ident = ids[at * 8 + piece]
            owner = ident >> 7
            slot = ident & 127
            flow = owner // sectors
            sector = owner - flow * sectors
            moving = flow != me
            rank = jnp.where(moving, count[flow], 0)
            count[flow] = rank + 1
            labels[jnp.where(moving, flow * CAP + rank, CAP * peers)] = slot + 1
            places.append(
                (flow * PEER_ROWS + rank * BLOCK_ROWS, (at * 8 + piece) * BLOCK_ROWS)
            )
            one_axial = len_axial[flow * 4 + (slot >> 5)]
            one_azim = len_azim[sector * 4 + ((slot >> 3) & 3)]
            one_radial = table[pl.ds(slot & 7, 1), :]
            if piece == 0:
                axial = jnp.full((ROWS, 128), one_axial, F32)
                azim = jnp.full((ROWS, 128), one_azim, F32)
                radial = jnp.broadcast_to(one_radial, (ROWS, 128))
            else:
                axial = jnp.where(group == piece, one_axial, axial)
                azim = jnp.where(group == piece, one_azim, azim)
                radial = jnp.where(group == piece, one_radial, radial)
        scales = [(-2.0 * DT) / length for length in (axial, azim, radial)]

        extrap = [
            [3.0 * (level(0, comp, t) - level(1, comp, t)) + level(2, comp, t) for t in range(8)]
            for comp in range(3)
        ]
        wind = [[scales[axis] * extrap[axis][t] for t in range(8)] for axis in range(3)]
        spin = []
        for k in range(4):
            value = jnp.zeros((ROWS, 128), F32)
            for c in range(4):
                value = jnp.where(c_at == c, F32(SLOPE[c, (c + k) % 4]), value)
            spin.append(value)
        same = [[pattern(SLOPE[2 * p, 2 * o], SLOPE[2 * p + 1, 2 * o + 1]) for o in range(2)] for p in range(2)]
        cross = [[pattern(SLOPE[2 * p, 2 * o + 1], SLOPE[2 * p + 1, 2 * o]) for o in range(2)] for p in range(2)]
        for comp in range(3):
            ue = extrap[comp]
            flipped = [subs(ue[t], 4) for t in range(8)]
            along_a = [None] * 8
            for half in range(2):
                for a, value in enumerate(slope_along([ue[2 * o + half] for o in range(4)])):
                    along_a[2 * a + half] = value
            tiles = []
            for t in range(8):
                a, half = t // 2, t % 2
                along_b = (
                    same[half][0] * ue[2 * a]
                    + cross[half][0] * flipped[2 * a]
                    + same[half][1] * ue[2 * a + 1]
                    + cross[half][1] * flipped[2 * a + 1]
                )
                along_c = spin[0] * ue[t]
                for k in range(1, 4):
                    along_c = along_c + spin[k] * subs(jnp.where(c_at < k, flipped[t], ue[t]), -k)
                advect = wind[0][t] * along_a[t] + wind[1][t] * along_b + wind[2][t] * along_c
                base = ue[t] + 1.5 * level(1, comp, t) - F32(2.0 / 3.0) * level(2, comp, t)
                tiles.append(base + advect)
            for (to_send, to_keep), tile in zip(places, swap_groups(tiles, group)):
                send[pl.ds(pl.multiple_of(to_send + comp * ROWS, ROWS), ROWS), :] = tile
                keep[pl.ds(pl.multiple_of(to_keep + comp * ROWS, ROWS), ROWS), :] = tile

    @pl.loop(0, CHUNKS)
    def _(n):
        chunk(n).wait()
        for k in range(columns):
            column(n * columns + k)
        kept(n).start()

    corner = sub == 0
    for t in range(peers):
        marks = jnp.zeros((ROWS, 128), jnp.int32)
        for rank in range(CAP):
            marks = jnp.where(corner & (lane == CAP * me + rank), labels[t * CAP + rank], marks)
        send[pl.ds(t * PEER_ROWS + CAP * BLOCK_ROWS, ROWS), :] = marks.astype(F32)
    leaving = pltpu.make_async_copy(send, send_h, small_sem.at[0])
    leaving.start()
    for n in range(CHUNKS):
        kept(n).wait()
    leaving.wait()


def at(a, b, c, h):
    return pl.ds((a * 16 + b * 4 + c) * 16 + h * ROWS, ROWS)


def join_radial(line, lane):
    first = line[0] + jnp.where(lane == 0, 0.0, lanes(line[3], 1))
    last = jnp.where(lane == 127, 0.0, lanes(first, -1))
    return [first, line[1], line[2], last]


def join_azim(ref, sub):
    ey = sub & 3
    for a in range(4):
        for c in range(4):
            for h in range(2):
                low = ref[at(a, 0, c, h), :]
                high = ref[at(a, 3, c, h), :]
                ref[at(a, 0, c, h), :] = low + jnp.where(ey == 0, 0.0, subs(high, 1))
                ref[at(a, 3, c, h), :] = high + jnp.where(ey == 3, 0.0, subs(low, -1))


def join_axial(ref, b, c, sub):
    top = sub < 4
    low = [ref[at(0, b, c, h), :] for h in range(2)]
    high = [ref[at(3, b, c, h), :] for h in range(2)]
    low_turned = [subs(x, 4) for x in low]
    high_turned = [subs(x, 4) for x in high]
    new_low = [
        low[0] + jnp.where(top, 0.0, high_turned[0]),
        low[1] + jnp.where(top, high_turned[0], high_turned[1]),
    ]
    new_high = [
        high[0] + jnp.where(top, low_turned[0], low_turned[1]),
        high[1] + jnp.where(top, low_turned[1], 0.0),
    ]
    return new_low, new_high


def lengths(len_axial, len_azim, len_radial, sub):
    slab = lax.axis_index("stream")
    sector = lax.axis_index("azim")
    columns, rows = len_axial.shape[0], len_azim.shape[0]
    x0, y0 = slab * 4, sector * 4
    top = sub < 4
    axial = [jnp.where(top, len_axial[x0 + 2 * h], len_axial[x0 + 2 * h + 1]) for h in range(2)]
    azim = choose(sub & 3, [jnp.full((ROWS, 128), len_azim[y0 + k], F32) for k in range(4)])
    radial = jnp.broadcast_to(len_radial[...], (ROWS, 128))
    before = len_axial[jnp.maximum(x0 - 1, 0)]
    after = len_axial[jnp.minimum(x0 + 4, columns - 1)]
    below = len_azim[lax.rem(y0 + rows - 1, rows)]
    above = len_azim[lax.rem(y0 + 4, rows)]
    return axial, azim, radial, (before, after, below, above)


def give(near, far, row, even, up, down):
    near[pl.ds(row, ROWS), :] = jnp.where(even, up, down)
    far[pl.ds(row, ROWS), :] = jnp.where(even, down, up)


def take(near, far, row, even):
    one, two = near[pl.ds(row, ROWS), :], far[pl.ds(row, ROWS), :]
    return jnp.where(even, two, one), jnp.where(even, one, two)


def load_kernel(
    ids, len_axial, len_azim, len_radial, solid, arrived, keep, pred, part, near, far,
    marks, marks_s, source, sem,
):
    lane, sub = iotas()
    group = lane >> 4
    peers = arrived.shape[0] // PEER_ROWS
    total = None
    for t in range(peers):
        tile = arrived[pl.ds(t * PEER_ROWS + CAP * BLOCK_ROWS, ROWS), :]
        total = tile if total is None else total + tile
    marks[...] = total.astype(jnp.int32)
    scalars = pltpu.make_async_copy(marks, marks_s, sem)
    scalars.start()
    slab, sectors = lax.axis_index("stream"), lax.axis_size("azim")
    for p in range(ids.shape[0]):
        ident = ids[p]
        stays = (ident >> 7) // sectors == slab
        source[jnp.where(stays, ident & 127, 128)] = -1 - p * BLOCK_ROWS
    scalars.wait()
    for n in range(peers * CAP):
        label = marks_s[0, n]
        source[jnp.where(label > 0, label - 1, 128)] = (
            (n // CAP) * PEER_ROWS + (n % CAP) * BLOCK_ROWS
        )

    def unpack(j, carry):
        places = [source[j * 8 + g] for g in range(8)]
        for comp in range(3):
            tiles = []
            for g, place in enumerate(places):
                row = pl.multiple_of(jnp.maximum(-1 - place, 0) + comp * ROWS, ROWS)
                kept = keep[pl.ds(row, ROWS), :]
                row = pl.multiple_of(jnp.maximum(place, 0) + comp * ROWS, ROWS)
                tiles.append(jnp.where(place >= 0, arrived[pl.ds(row, ROWS), :], kept))
            for t, tile in enumerate(swap_groups(tiles, group)):
                pred[pl.ds(comp * 1024 + 8 * t * 16 + j, ROWS, stride=16), :] = tile
        return carry

    lax.fori_loop(0, 16, unpack, 0, unroll=4)

    axial, azim, radial, _ = lengths(len_axial, len_azim, len_radial, sub)
    inverse = [
        1.0 / (F32(11.0 / 6.0) + F32(DT * PENALTY) * solid[pl.ds(h * ROWS, ROWS), :].astype(F32))
        for h in range(2)
    ]

    def scaled(comp, a, b, c, h):
        spot = pl.ds(comp * 1024 + (a * 16 + b * 4 + c) * 16 + h * ROWS, ROWS)
        value = pred[spot, :] * inverse[h]
        pred[spot, :] = value
        return value

    area = [
        [0.25 * azim * radial for h in range(2)],
        [0.25 * axial[h] * radial for h in range(2)],
        [0.25 * axial[h] * azim for h in range(2)],
    ]
    for h in range(2):
        for b in range(4):
            for c in range(4):
                line = [scaled(0, a, b, c, h) for a in range(4)]
                for a, value in enumerate(slope_along(line)):
                    part[at(a, b, c, h), :] = area[0][h] * value
        for a in range(4):
            for c in range(4):
                line = [scaled(1, a, b, c, h) for b in range(4)]
                for b, value in enumerate(slope_along(line)):
                    part[at(a, b, c, h), :] += area[1][h] * value
        for a in range(4):
            for b in range(4):
                line = [scaled(2, a, b, c, h) for c in range(4)]
                line = [
                    float(-WEIGHT[a] * WEIGHT[b] * WEIGHT[c])
                    * (part[at(a, b, c, h), :] + area[2][h] * value)
                    for c, value in enumerate(slope_along(line))
                ]
                for c, value in enumerate(join_radial(line, lane)):
                    part[at(a, b, c, h), :] = value
    join_azim(part, sub)
    top = sub < 4
    even = lax.rem(slab, 2) == 0
    for b in range(4):
        for c in range(4):
            low, high = join_axial(part, b, c, sub)
            for h in range(2):
                part[at(0, b, c, h), :] = low[h]
                part[at(3, b, c, h), :] = high[h]
            inner = [[part[at(a, b, c, h), :] for a in (1, 2)] for h in range(2)]
            normal = combine(STIFF[3], [low[1], *inner[1], high[1]])
            up = jnp.where(top, subs(high[1], 4), normal)
            normal = combine(STIFF[0], [low[0], *inner[0], high[0]])
            down = jnp.where(top, low[0], subs(normal, 4))
            give(near, far, (b * 4 + c) * ROWS, even, up, down)


def axial_kernel(part, near_in, far_in, field, normals, near, far):
    lane, sub = iotas()
    top = sub < 4
    slab = lax.axis_index("stream")
    first = jnp.where(slab == 0, F32(0.0), F32(1.0))
    last = jnp.where(slab == lax.axis_size("stream") - 1, F32(0.0), F32(1.0))
    even = lax.rem(slab, 2) == 0
    for b in range(4):
        for c in range(4):
            spot = pl.ds((b * 4 + c) * ROWS, ROWS)
            low = part[at(0, b, c, 0), :]
            high = part[at(3, b, c, 1), :]
            under, over = take(near_in, far_in, (b * 4 + c) * ROWS, even)
            normals[spot, :] = jnp.where(
                top,
                subs(under, 4) + float(STIFF[3, 3]) * low,
                over + float(STIFF[0, 0]) * high,
            )
            field[at(0, b, c, 0), :] = low + jnp.where(top, first * under, 0.0)
            field[at(3, b, c, 1), :] = jnp.where(top, high, last * (high + subs(over, 4)))
            field[at(0, b, c, 1), :] = part[at(0, b, c, 1), :]
            field[at(3, b, c, 0), :] = part[at(3, b, c, 0), :]
            for a in (1, 2):
                for h in range(2):
                    field[at(a, b, c, h), :] = part[at(a, b, c, h), :]
    ey = sub & 3
    even = lax.rem(lax.axis_index("azim"), 2) == 0
    for a in range(4):
        for c in range(4):
            line = [[field[at(a, b, c, h), :] for b in range(4)] for h in range(2)]
            normal = [combine(STIFF[3], line[h]) for h in range(2)]
            up = choose(
                ey, [subs(normal[1], -3), subs(normal[0], -2), subs(line[1][3], -1), line[0][3]]
            )
            normal = [combine(STIFF[0], line[h]) for h in range(2)]
            down = choose(
                ey, [line[0][0], subs(line[1][0], 1), subs(normal[0], 2), subs(normal[1], 3)]
            )
            give(near, far, (a * 4 + c) * ROWS, even, up, down)
    edge = [normals[pl.ds((12 + c) * ROWS, ROWS), :] for c in range(4)]
    up = choose(ey, [subs(edge[3], -3), subs(edge[2], -2), subs(edge[1], -1), edge[0]])
    edge = [normals[pl.ds(c * ROWS, ROWS), :] for c in range(4)]
    down = choose(ey, [edge[0], subs(edge[1], 1), subs(edge[2], 2), subs(edge[3], 3)])
    give(near, far, 16 * ROWS, even, up, down)


def image_kernel(
    len_axial, len_azim, len_radial, part, normals_in, near, far, field, image, sums, normals, sides
):
    lane, sub = iotas()
    top = sub < 4
    ey = sub & 3
    slab = lax.axis_index("stream")
    first = jnp.where(slab == 0, F32(0.0), F32(1.0))
    last = jnp.where(slab == lax.axis_size("stream") - 1, F32(0.0), F32(1.0))
    even = lax.rem(lax.axis_index("azim"), 2) == 0
    for a in range(4):
        for c in range(4):
            under, over = take(near, far, (a * 4 + c) * ROWS, even)
            under_face = [subs(under, -3), subs(under, -2)]
            under_normal = [subs(under, -1), under]
            over_face = [subs(over, 3), subs(over, 2)]
            over_normal = [subs(over, 1), over]
            for h in range(2):
                low = part[at(a, 0, c, h), :]
                high = part[at(a, 3, c, h), :]
                sides[pl.ds(((a * 4 + c) * 2 + h) * ROWS, ROWS), :] = jnp.where(
                    ey == 0,
                    under_normal[h] + float(STIFF[3, 3]) * low,
                    over_normal[h] + float(STIFF[0, 0]) * high,
                )
                field[at(a, 0, c, h), :] = low + jnp.where(ey == 0, under_face[h], 0.0)
                field[at(a, 3, c, h), :] = high + jnp.where(ey == 3, over_face[h], 0.0)
                for b in (1, 2):
                    field[at(a, b, c, h), :] = part[at(a, b, c, h), :]
    under, over = take(near, far, 16 * ROWS, even)
    for c in range(4):
        spot = pl.ds(c * ROWS, ROWS)
        normals[spot, :] = normals_in[spot, :] + jnp.where(ey == 0, subs(under, c - 3), 0.0)
        spot = pl.ds((12 + c) * ROWS, ROWS)
        normals[spot, :] = normals_in[spot, :] + jnp.where(ey == 3, subs(over, 3 - c), 0.0)
        for b in (1, 2):
            spot = pl.ds((b * 4 + c) * ROWS, ROWS)
            normals[spot, :] = normals_in[spot, :]

    axial, azim, radial, (before, after, beneath, beyond) = lengths(
        len_axial, len_azim, len_radial, sub
    )
    zero = jnp.zeros((ROWS, 128), F32)
    rx = [2.0 / axial[h] for h in range(2)]
    ry = 2.0 / azim
    rz = 2.0 / radial
    qz = 0.5 * radial
    qx = [[0.5 * axial[h] for a in range(4)] for h in range(2)]
    before_v, after_v = jnp.full((ROWS, 128), before, F32), jnp.full((ROWS, 128), after, F32)
    beneath_v, beyond_v = jnp.full((ROWS, 128), beneath, F32), jnp.full((ROWS, 128), beyond, F32)
    own_x = [qx[h][0] for h in range(2)]
    qx[0][0] = own_x[0] + jnp.where(top, first * 0.5 * before_v, 0.0)
    qx[1][3] = own_x[1] + jnp.where(top, 0.0, last * 0.5 * after_v)
    ghost_x = [jnp.where(top, first * 2.0 / before_v, 0.0), jnp.where(top, 0.0, last * 2.0 / after_v)]
    own_y = 0.5 * azim
    qy = [
        own_y + jnp.where(ey == 0, 0.5 * beneath_v, 0.0),
        own_y,
        own_y,
        own_y + jnp.where(ey == 3, 0.5 * beyond_v, 0.0),
    ]
    ghost_y = [jnp.where(ey == 0, 2.0 / beneath_v, 0.0), zero, zero, jnp.where(ey == 3, 2.0 / beyond_v, 0.0)]

    for h in range(2):
        factor = [rx[h] * qz * qy[b] for b in range(4)]
        extra = [ghost_x[h] * qz * qy[b] for b in range(4)]
        edge_a = 0 if h == 0 else 3
        for b in range(4):
            for c in range(4):
                line = [field[at(a, b, c, h), :] for a in range(4)]
                for a, value in enumerate(stiff_along(line)):
                    value = factor[b] * value
                    if a == edge_a:
                        value = value + extra[b] * normals[pl.ds((b * 4 + c) * ROWS, ROWS), :]
                    image[at(a, b, c, h), :] = float(WEIGHT[b] * WEIGHT[c]) * value
        for a in range(4):
            factor_a = ry * qz * qx[h][a]
            extra_a = [ghost_y[b] * qz * qx[h][a] for b in range(4)]
            for c in range(4):
                line = [field[at(a, b, c, h), :] for b in range(4)]
                side = sides[pl.ds(((a * 4 + c) * 2 + h) * ROWS, ROWS), :]
                for b, value in enumerate(stiff_along(line)):
                    value = factor_a * value
                    if b in (0, 3):
                        value = value + extra_a[b] * side
                    image[at(a, b, c, h), :] += float(WEIGHT[a] * WEIGHT[c]) * value
        for a in range(4):
            for b in range(4):
                factor_ab = (float(WEIGHT[a] * WEIGHT[b]) * rz) * qx[h][a] * qy[b]
                line = [field[at(a, b, c, h), :] for c in range(4)]
                line = [
                    image[at(a, b, c, h), :] + factor_ab * value
                    for c, value in enumerate(stiff_along(line))
                ]
                for c, value in enumerate(join_radial(line, lane)):
                    image[at(a, b, c, h), :] = value
    join_azim(image, sub)
    outlet = jnp.where(top, 1.0, last)
    for b in range(4):
        for c in range(4):
            low, high = join_axial(image, b, c, sub)
            high[1] = high[1] * outlet
            for h in range(2):
                image[at(0, b, c, h), :] = low[h]
                image[at(3, b, c, h), :] = high[h]

    load_load = load_image = image_image = zero
    for h in range(2):
        for a in range(3):
            for b in range(3):
                for c in range(3):
                    one, two = field[at(a, b, c, h), :], image[at(a, b, c, h), :]
                    load_load = load_load + one * one
                    load_image = load_image + one * two
                    image_image = image_image + two * two
    energy = zero
    for h in range(2):
        along = [zero, zero, zero]
        for m in range(4):
            for n in range(4):
                weight = float(WEIGHT[m] * WEIGHT[n])
                lines = (
                    [image[at(k, m, n, h), :] for k in range(4)],
                    [image[at(m, k, n, h), :] for k in range(4)],
                    [image[at(m, n, k, h), :] for k in range(4)],
                )
                for axis, line in enumerate(lines):
                    dot = None
                    for one, two in zip(line, stiff_along(line)):
                        term = one * two
                        dot = term if dot is None else dot + term
                    along[axis] = along[axis] + weight * dot
        energy = (
            energy
            + rx[h] * own_y * qz * along[0]
            + ry * own_x[h] * qz * along[1]
            + rz * own_x[h] * own_y * along[2]
        )
    row = zero
    for k, value in enumerate((load_load, load_image, image_image, energy)):
        value = jnp.sum(jnp.sum(value, axis=0, keepdims=True), axis=1, keepdims=True)
        row = jnp.where(lane == k, jnp.broadcast_to(value, (ROWS, 128)), row)
    for k in range(sums.shape[0] // ROWS):
        sums[pl.ds(k * ROWS, ROWS), :] = row


def final_kernel(
    len_axial, len_azim, len_radial, sums, field, image, pred, velocity_h, pressure_h, velocity, pressure, sems
):
    lane, sub = iotas()
    total = sums[pl.ds(0, ROWS), :]
    for k in range(1, sums.shape[0] // ROWS):
        total = total + sums[pl.ds(k * ROWS, ROWS), :]
    total = jnp.broadcast_to(jnp.sum(total, axis=0, keepdims=True), (ROWS, 128))
    s0, s1, s2, s3 = (
        jnp.broadcast_to(
            jnp.sum(jnp.where(lane == k, total, 0.0), axis=1, keepdims=True), (ROWS, 128)
        )
        for k in range(4)
    )
    alpha = s0 / s1
    ratio = s2 / s1
    grown = alpha * ratio
    energy = alpha * (s3 - s2 * ratio)
    second = s0 * (grown - 1.0) / (alpha * energy)
    of_load = alpha + second * grown
    of_image = -(second * alpha)

    axial, azim, radial, _ = lengths(len_axial, len_azim, len_radial, sub)
    for h in range(2):
        for a in range(4):
            for b in range(4):
                for c in range(4):
                    spot = at(a, b, c, h)
                    pressure[spot, :] = of_load * field[spot, :] + of_image * image[spot, :]
    leaving = [pltpu.make_async_copy(pressure, pressure_h, sems.at[3])]
    leaving[0].start()
    for axis in range(3):
        for h in range(2):
            scale = 2.0 / (axial[h], azim, radial)[axis]
            for m in range(4):
                for n in range(4):
                    line = [(k, m, n) if axis == 0 else (m, k, n) if axis == 1 else (m, n, k) for k in range(4)]
                    values = slope_along([pressure[at(*node, h), :] for node in line])
                    for (a, b, c), value in zip(line, values):
                        spot = pl.ds(axis * 1024 + (a * 16 + b * 4 + c) * 16 + h * ROWS, ROWS)
                        velocity[spot, :] = pred[spot, :] - scale * value
        span = pl.ds(axis * 1024, 1024)
        leaving.append(pltpu.make_async_copy(velocity.at[span, :], velocity_h.at[span, :], sems.at[axis]))
        leaving[-1].start()
    for copy in leaving:
        copy.wait()


SMEM = pl.BlockSpec(memory_space=pltpu.SMEM)
VMEM = pl.BlockSpec(memory_space=pltpu.VMEM)
HBM = pl.BlockSpec(memory_space=pltpu.HBM)


def array(rows, kind=F32):
    return jax.ShapeDtypeStruct((rows, 128), kind)


def call(kernel, ins, outs, scratch, name, place=VMEM, limit=VMEM_LIMIT):
    return pl.pallas_call(
        kernel,
        out_shape=outs,
        in_specs=ins,
        out_specs=[place] * len(outs),
        scratch_shapes=scratch,
        compiler_params=pltpu.CompilerParams(vmem_limit_bytes=limit),
        name=name,
    )


def swapped(axis, near, far, closed):
    count = lax.axis_size(axis)
    apart = [(i + 1) % count if i % 2 else (i - 1) % count for i in range(count)]
    if not closed:
        apart[0], apart[-1] = 0, count - 1
    far = lax.ppermute(far, axis, list(enumerate(apart)))
    return lax.ppermute(near, axis, [(i, i ^ 1) for i in range(count)]), far


def body(history, block_ids, len_axial, len_azim, len_radial, solid):
    slabs, sectors = lax.axis_size("stream"), lax.axis_size("azim")
    radial = len_radial.reshape(1, 128)
    geometry = (len_axial, len_azim, radial)
    geometry_specs = [SMEM, SMEM, VMEM]
    hist = history.reshape(576, history.shape[3])
    send, keep = call(
        pack_kernel,
        [HBM] * 5,
        [array(slabs * PEER_ROWS), array(128 * BLOCK_ROWS)],
        [
            pltpu.VMEM(hist.shape, F32),
            pltpu.VMEM((slabs * PEER_ROWS, 128), F32),
            pltpu.VMEM((128 * BLOCK_ROWS, 128), F32),
            pltpu.SMEM(block_ids.shape, jnp.int32),
            pltpu.SMEM(len_axial.shape, F32),
            pltpu.SMEM(len_azim.shape, F32),
            pltpu.VMEM((1, 128), F32),
            pltpu.SMEM((slabs,), jnp.int32),
            pltpu.SMEM((CAP * slabs + 1,), jnp.int32),
            pltpu.VMEM((ROWS, 128), F32),
            pltpu.SemaphoreType.DMA((CHUNKS,)),
            pltpu.SemaphoreType.DMA((CHUNKS,)),
            pltpu.SemaphoreType.DMA((4,)),
        ],
        "pack",
        HBM,
        limit=PACK_LIMIT,
    )(block_ids, *geometry, hist)
    arrived = lax.all_to_all(
        send.reshape(slabs, PEER_ROWS, 128), "stream", split_axis=0, concat_axis=0, tiled=True
    ).reshape(slabs * PEER_ROWS, 128)
    pred, part, near, far = call(
        load_kernel,
        [SMEM] + geometry_specs + [VMEM] * 3,
        [array(3 * 1024), array(1024), array(128), array(128)],
        [
            pltpu.VMEM((ROWS, 128), jnp.int32),
            pltpu.SMEM((ROWS, 128), jnp.int32),
            pltpu.SMEM((129,), jnp.int32),
            pltpu.SemaphoreType.DMA(()),
        ],
        "load",
    )(block_ids, *geometry, solid.reshape(16, 128), arrived, keep)
    near, far = swapped("stream", near, far, False)
    part, normals, near, far = call(
        axial_kernel,
        [VMEM] * 3,
        [array(1024), array(128), array(136), array(136)],
        [],
        "axial_faces",
    )(part, near, far)
    near, far = swapped("azim", near, far, True)
    field, image, sums = call(
        image_kernel,
        geometry_specs + [VMEM] * 4,
        [array(1024), array(1024), array(slabs * sectors)],
        [pltpu.VMEM((128, 128), F32), pltpu.VMEM((256, 128), F32)],
        "image",
    )(*geometry, part, normals, near, far)
    sums = lax.all_to_all(
        sums.reshape(slabs * sectors, 1, 128),
        ("stream", "azim"),
        split_axis=0,
        concat_axis=0,
        tiled=True,
    ).reshape(slabs * sectors, 128)
    velocity, pressure = call(
        final_kernel,
        geometry_specs + [VMEM] * 4,
        [array(3 * 1024), array(1024)],
        [
            pltpu.VMEM((3 * 1024, 128), F32),
            pltpu.VMEM((1024, 128), F32),
            pltpu.SemaphoreType.DMA((4,)),
        ],
        "velocity",
        HBM,
    )(*geometry, sums, field, image, pred)
    return velocity.reshape(3, 4, 4, 4, 4, 4, 128), pressure.reshape(4, 4, 4, 4, 4, 128)


def solution(mesh):
    in_specs = (
        P(None, None, None, ("stream", "azim")),
        P(("stream", "azim")),
        P(),
        P(),
        P(),
        P("stream", "azim", None),
    )
    out_specs = (
        P(None, None, None, None, "stream", "azim", None),
        P(None, None, None, "stream", "azim", None),
    )
    return jax.shard_map(body, mesh=mesh, in_specs=in_specs, out_specs=out_specs, check_vma=False)
```

```python
import functools
import math

import jax
import jax.numpy as jnp
import numpy as np
from jax import lax
from jax.experimental import pallas as pl
from jax.experimental.pallas import tpu as pltpu
from jax.sharding import PartitionSpec as P

CAP = 2
DT = 0.01
PENALTY = 100.0
VMEM_LIMIT = 40 * 1024 * 1024
PACK_LIMIT = 60 * 1024 * 1024
F32 = jnp.float32


def node_tables():
    root = 1.0 / math.sqrt(5.0)
    points = np.array([-1.0, -root, root, 1.0])
    weights = np.array([1.0 / 6.0, 5.0 / 6.0, 5.0 / 6.0, 1.0 / 6.0])
    legendre = (5.0 * points**3 - 3.0 * points) / 2.0
    slope = np.zeros((4, 4))
    for first in range(4):
        for second in range(4):
            if first != second:
                slope[first, second] = legendre[first] / (
                    legendre[second] * (points[first] - points[second])
                )
    slope[0, 0] = -3.0
    slope[3, 3] = 3.0
    return slope, weights


SLOPE, WEIGHT = node_tables()
STIFF = SLOPE.T @ np.diag(WEIGHT) @ SLOPE
EDGE = float(WEIGHT[0])

ROWS = 8
BLOCK_ROWS = 24
PEER_ROWS = CAP * BLOCK_ROWS + ROWS


def iotas():
    lane = lax.broadcasted_iota(jnp.int32, (ROWS, 128), 1)
    sub = lax.broadcasted_iota(jnp.int32, (ROWS, 128), 0)
    return lane, sub


def lanes(x, shift):
    shift %= 128
    return pltpu.roll(x, shift, 1) if shift else x


def subs(x, shift):
    shift %= ROWS
    return pltpu.roll(x, shift, 0) if shift else x


def combine(coefs, values, factor=1.0):
    total = None
    for coef, value in zip(coefs, values):
        coef = factor * float(coef)
        term = coef * value
        total = term if total is None else total + term
    return total


def halves(line):
    return (line[0] + line[3], line[1] + line[2]), (line[0] - line[3], line[1] - line[2])


def slope_along(line):
    even, odd = halves(line)
    first = [combine(SLOPE[i, :2] - SLOPE[i, :1:-1], odd, 0.5) for i in range(2)]
    second = [combine(SLOPE[i, :2] + SLOPE[i, :1:-1], even, 0.5) for i in range(2)]
    return [first[0] + second[0], first[1] + second[1], first[1] - second[1], first[0] - second[0]]


def stiff_along(line):
    even, odd = halves(line)
    first = [combine(STIFF[i, :2] + STIFF[i, :1:-1], even, 0.5) for i in range(2)]
    second = [combine(STIFF[i, :2] - STIFF[i, :1:-1], odd, 0.5) for i in range(2)]
    return [first[0] + second[0], first[1] + second[1], first[1] - second[1], first[0] - second[0]]


def choose(key, values):
    result = values[0]
    for at in range(1, len(values)):
        result = jnp.where(key == at, values[at], result)
    return result


def swap_groups(tiles, group):
    mixed = [lanes(tile, 16 * t) for t, tile in enumerate(tiles)]
    for bit in (1, 2, 4):
        odd = (group & bit) != 0
        mixed = [jnp.where(odd, mixed[(t + bit) & 7], mixed[t]) for t in range(8)]
    return [lanes(mixed[-g & 7], -16 * g) for g in range(8)]


CHUNKS = 4


def pack_kernel(
    ids_h, axial_h, azim_h, radial_h, hist_h, send_h, keep_h,
    hist, send, keep, ids, len_axial, len_azim, len_radial, count, labels, table,
    hist_sem, keep_sem, small_sem,
):
    sectors = lax.axis_size("azim")
    peers = lax.axis_size("stream")
    me = lax.axis_index("stream")
    width = hist.shape[1] // CHUNKS
    columns = width // 128

    def chunk(n):
        span = pl.ds(pl.multiple_of(n * width, width), width)
        return pltpu.make_async_copy(hist_h.at[:, span], hist.at[:, span], hist_sem.at[n])

    def kept(n):
        rows = keep.shape[0] // CHUNKS
        span = pl.ds(pl.multiple_of(n * rows, rows), rows)
        return pltpu.make_async_copy(keep.at[span, :], keep_h.at[span, :], keep_sem.at[n])

    small = [
        pltpu.make_async_copy(source, target, small_sem.at[n])
        for n, (source, target) in enumerate(
            ((ids_h, ids), (axial_h, len_axial), (azim_h, len_azim), (radial_h, len_radial))
        )
    ]
    for copy in small:
        copy.start()
    for n in range(CHUNKS):
        chunk(n).start()
    lane, sub = iotas()
    group = lane >> 4
    c_at = sub & 3
    for t in range(peers):
        count[t] = 0
    for n in range(CAP * peers):
        labels[n] = 0
    for copy in small:
        copy.wait()
    whole = jnp.broadcast_to(len_radial[...], (ROWS, 128))
    rows = choose(sub, [lanes(whole, -16 * z) for z in range(8)])
    rows = jnp.where(group == 0, rows, 0.0)
    for shift in (16, 32, 64):
        rows = rows + lanes(rows, shift)
    table[...] = rows

    def pattern(low, high):
        return jnp.where(sub < 4, F32(low), F32(high))

    def column(at):
        offset = pl.multiple_of(at * 128, 128)

        def level(which, comp, t):
            return hist[pl.ds((which * 3 + comp) * 64 + 8 * t, ROWS), pl.ds(offset, 128)]

        places = []
        axial = azim = radial = None
        for piece in range(8):
            ident = ids[at * 8 + piece]
            owner = ident >> 7
            slot = ident & 127
            flow = owner // sectors
            sector = owner - flow * sectors
            moving = flow != me
            rank = jnp.where(moving, count[flow], 0)
            count[flow] = rank + 1
            labels[jnp.where(moving, flow * CAP + rank, CAP * peers)] = slot + 1
            places.append(
                (flow * PEER_ROWS + rank * BLOCK_ROWS, (at * 8 + piece) * BLOCK_ROWS)
            )
            one_axial = len_axial[flow * 4 + (slot >> 5)]
            one_azim = len_azim[sector * 4 + ((slot >> 3) & 3)]
            one_radial = table[pl.ds(slot & 7, 1), :]
            if piece == 0:
                axial = jnp.full((ROWS, 128), one_axial, F32)
                azim = jnp.full((ROWS, 128), one_azim, F32)
                radial = jnp.broadcast_to(one_radial, (ROWS, 128))
            else:
                axial = jnp.where(group == piece, one_axial, axial)
                azim = jnp.where(group == piece, one_azim, azim)
                radial = jnp.where(group == piece, one_radial, radial)
        scales = [(-2.0 * DT) / length for length in (axial, azim, radial)]

        extrap = [
            [3.0 * (level(0, comp, t) - level(1, comp, t)) + level(2, comp, t) for t in range(8)]
            for comp in range(3)
        ]
        wind = [[scales[axis] * extrap[axis][t] for t in range(8)] for axis in range(3)]
        spin = []
        for k in range(4):
            value = jnp.zeros((ROWS, 128), F32)
            for c in range(4):
                value = jnp.where(c_at == c, F32(SLOPE[c, (c + k) % 4]), value)
            spin.append(value)
        same = [[pattern(SLOPE[2 * p, 2 * o], SLOPE[2 * p + 1, 2 * o + 1]) for o in range(2)] for p in range(2)]
        cross = [[pattern(SLOPE[2 * p, 2 * o + 1], SLOPE[2 * p + 1, 2 * o]) for o in range(2)] for p in range(2)]
        for comp in range(3):
            ue = extrap[comp]
            flipped = [subs(ue[t], 4) for t in range(8)]
            along_a = [None] * 8
            for half in range(2):
                for a, value in enumerate(slope_along([ue[2 * o + half] for o in range(4)])):
                    along_a[2 * a + half] = value
            tiles = []
            for t in range(8):
                a, half = t // 2, t % 2
                along_b = (
                    same[half][0] * ue[2 * a]
                    + cross[half][0] * flipped[2 * a]
                    + same[half][1] * ue[2 * a + 1]
                    + cross[half][1] * flipped[2 * a + 1]
                )
                along_c = spin[0] * ue[t]
                for k in range(1, 4):
                    along_c = along_c + spin[k] * subs(jnp.where(c_at < k, flipped[t], ue[t]), -k)
                advect = wind[0][t] * along_a[t] + wind[1][t] * along_b + wind[2][t] * along_c
                base = ue[t] + 1.5 * level(1, comp, t) - F32(2.0 / 3.0) * level(2, comp, t)
                tiles.append(base + advect)
            for (to_send, to_keep), tile in zip(places, swap_groups(tiles, group)):
                send[pl.ds(pl.multiple_of(to_send + comp * ROWS, ROWS), ROWS), :] = tile
                keep[pl.ds(pl.multiple_of(to_keep + comp * ROWS, ROWS), ROWS), :] = tile

    @pl.loop(0, CHUNKS)
    def _(n):
        chunk(n).wait()
        for k in range(columns):
            column(n * columns + k)
        kept(n).start()

    corner = sub == 0
    for t in range(peers):
        marks = jnp.zeros((ROWS, 128), jnp.int32)
        for rank in range(CAP):
            marks = jnp.where(corner & (lane == CAP * me + rank), labels[t * CAP + rank], marks)
        send[pl.ds(t * PEER_ROWS + CAP * BLOCK_ROWS, ROWS), :] = marks.astype(F32)
    leaving = pltpu.make_async_copy(send, send_h, small_sem.at[0])
    leaving.start()
    for n in range(CHUNKS):
        kept(n).wait()
    leaving.wait()


def at(a, b, c, h):
    return pl.ds((a * 16 + b * 4 + c) * 16 + h * ROWS, ROWS)


def join_radial(line, lane):
    first = line[0] + jnp.where(lane == 0, 0.0, lanes(line[3], 1))
    last = jnp.where(lane == 127, 0.0, lanes(first, -1))
    return [first, line[1], line[2], last]


def join_azim(ref, sub):
    ey = sub & 3
    for a in range(4):
        for c in range(4):
            for h in range(2):
                low = ref[at(a, 0, c, h), :]
                high = ref[at(a, 3, c, h), :]
                ref[at(a, 0, c, h), :] = low + jnp.where(ey == 0, 0.0, subs(high, 1))
                ref[at(a, 3, c, h), :] = high + jnp.where(ey == 3, 0.0, subs(low, -1))


def join_axial(ref, b, c, sub):
    top = sub < 4
    low = [ref[at(0, b, c, h), :] for h in range(2)]
    high = [ref[at(3, b, c, h), :] for h in range(2)]
    low_turned = [subs(x, 4) for x in low]
    high_turned = [subs(x, 4) for x in high]
    new_low = [
        low[0] + jnp.where(top, 0.0, high_turned[0]),
        low[1] + jnp.where(top, high_turned[0], high_turned[1]),
    ]
    new_high = [
        high[0] + jnp.where(top, low_turned[0], low_turned[1]),
        high[1] + jnp.where(top, low_turned[1], 0.0),
    ]
    return new_low, new_high


def lengths(len_axial, len_azim, len_radial, sub):
    slab = lax.axis_index("stream")
    sector = lax.axis_index("azim")
    columns, rows = len_axial.shape[0], len_azim.shape[0]
    x0, y0 = slab * 4, sector * 4
    top = sub < 4
    axial = [jnp.where(top, len_axial[x0 + 2 * h], len_axial[x0 + 2 * h + 1]) for h in range(2)]
    azim = choose(sub & 3, [jnp.full((ROWS, 128), len_azim[y0 + k], F32) for k in range(4)])
    radial = jnp.broadcast_to(len_radial[...], (ROWS, 128))
    before = len_axial[jnp.maximum(x0 - 1, 0)]
    after = len_axial[jnp.minimum(x0 + 4, columns - 1)]
    below = len_azim[lax.rem(y0 + rows - 1, rows)]
    above = len_azim[lax.rem(y0 + 4, rows)]
    return axial, azim, radial, (before, after, below, above)


def give(near, far, row, even, up, down):
    near[pl.ds(row, ROWS), :] = jnp.where(even, up, down)
    far[pl.ds(row, ROWS), :] = jnp.where(even, down, up)


def take(near, far, row, even):
    one, two = near[pl.ds(row, ROWS), :], far[pl.ds(row, ROWS), :]
    return jnp.where(even, two, one), jnp.where(even, one, two)


def load_kernel(
    ids, len_axial, len_azim, len_radial, solid, arrived, keep, pred, part, near, far,
    marks, marks_s, source, sem,
):
    lane, sub = iotas()
    group = lane >> 4
    peers = arrived.shape[0] // PEER_ROWS
    total = None
    for t in range(peers):
        tile = arrived[pl.ds(t * PEER_ROWS + CAP * BLOCK_ROWS, ROWS), :]
        total = tile if total is None else total + tile
    marks[...] = total.astype(jnp.int32)
    scalars = pltpu.make_async_copy(marks, marks_s, sem)
    scalars.start()
    slab, sectors = lax.axis_index("stream"), lax.axis_size("azim")
    for p in range(ids.shape[0]):
        ident = ids[p]
        stays = (ident >> 7) // sectors == slab
        source[jnp.where(stays, ident & 127, 128)] = -1 - p * BLOCK_ROWS
    scalars.wait()
    for n in range(peers * CAP):
        label = marks_s[0, n]
        source[jnp.where(label > 0, label - 1, 128)] = (
            (n // CAP) * PEER_ROWS + (n % CAP) * BLOCK_ROWS
        )

    def unpack(j, carry):
        places = [source[j * 8 + g] for g in range(8)]
        for comp in range(3):
            tiles = []
            for g, place in enumerate(places):
                row = pl.multiple_of(jnp.maximum(-1 - place, 0) + comp * ROWS, ROWS)
                kept = keep[pl.ds(row, ROWS), :]
                row = pl.multiple_of(jnp.maximum(place, 0) + comp * ROWS, ROWS)
                tiles.append(jnp.where(place >= 0, arrived[pl.ds(row, ROWS), :], kept))
            for t, tile in enumerate(swap_groups(tiles, group)):
                pred[pl.ds(comp * 1024 + 8 * t * 16 + j, ROWS, stride=16), :] = tile
        return carry

    lax.fori_loop(0, 16, unpack, 0, unroll=8)

    axial, azim, radial, _ = lengths(len_axial, len_azim, len_radial, sub)
    inverse = [
        1.0 / (F32(11.0 / 6.0) + F32(DT * PENALTY) * solid[pl.ds(h * ROWS, ROWS), :].astype(F32))
        for h in range(2)
    ]

    def scaled(comp, a, b, c, h):
        spot = pl.ds(comp * 1024 + (a * 16 + b * 4 + c) * 16 + h * ROWS, ROWS)
        value = pred[spot, :] * inverse[h]
        pred[spot, :] = value
        return value

    area = [
        [0.25 * azim * radial for h in range(2)],
        [0.25 * axial[h] * radial for h in range(2)],
        [0.25 * axial[h] * azim for h in range(2)],
    ]
    for h in range(2):
        for b in range(4):
            for c in range(4):
                line = [scaled(0, a, b, c, h) for a in range(4)]
                for a, value in enumerate(slope_along(line)):
                    part[at(a, b, c, h), :] = area[0][h] * value
        for a in range(4):
            for c in range(4):
                line = [scaled(1, a, b, c, h) for b in range(4)]
                for b, value in enumerate(slope_along(line)):
                    part[at(a, b, c, h), :] += area[1][h] * value
        for a in range(4):
            for b in range(4):
                line = [scaled(2, a, b, c, h) for c in range(4)]
                line = [
                    float(-WEIGHT[a] * WEIGHT[b] * WEIGHT[c])
                    * (part[at(a, b, c, h), :] + area[2][h] * value)
                    for c, value in enumerate(slope_along(line))
                ]
                for c, value in enumerate(join_radial(line, lane)):
                    part[at(a, b, c, h), :] = value
    join_azim(part, sub)
    top = sub < 4
    even = lax.rem(slab, 2) == 0
    for b in range(4):
        for c in range(4):
            low, high = join_axial(part, b, c, sub)
            for h in range(2):
                part[at(0, b, c, h), :] = low[h]
                part[at(3, b, c, h), :] = high[h]
            inner = [[part[at(a, b, c, h), :] for a in (1, 2)] for h in range(2)]
            normal = combine(STIFF[3], [low[1], *inner[1], high[1]])
            up = jnp.where(top, subs(high[1], 4), normal)
            normal = combine(STIFF[0], [low[0], *inner[0], high[0]])
            down = jnp.where(top, low[0], subs(normal, 4))
            give(near, far, (b * 4 + c) * ROWS, even, up, down)


def axial_kernel(part, near_in, far_in, field, normals, near, far):
    lane, sub = iotas()
    top = sub < 4
    slab = lax.axis_index("stream")
    first = jnp.where(slab == 0, F32(0.0), F32(1.0))
    last = jnp.where(slab == lax.axis_size("stream") - 1, F32(0.0), F32(1.0))
    even = lax.rem(slab, 2) == 0
    for b in range(4):
        for c in range(4):
            spot = pl.ds((b * 4 + c) * ROWS, ROWS)
            low = part[at(0, b, c, 0), :]
            high = part[at(3, b, c, 1), :]
            under, over = take(near_in, far_in, (b * 4 + c) * ROWS, even)
            normals[spot, :] = jnp.where(
                top,
                subs(under, 4) + float(STIFF[3, 3]) * low,
                over + float(STIFF[0, 0]) * high,
            )
            field[at(0, b, c, 0), :] = low + jnp.where(top, first * under, 0.0)
            field[at(3, b, c, 1), :] = jnp.where(top, high, last * (high + subs(over, 4)))
            field[at(0, b, c, 1), :] = part[at(0, b, c, 1), :]
            field[at(3, b, c, 0), :] = part[at(3, b, c, 0), :]
            for a in (1, 2):
                for h in range(2):
                    field[at(a, b, c, h), :] = part[at(a, b, c, h), :]
    ey = sub & 3
    even = lax.rem(lax.axis_index("azim"), 2) == 0
    for a in range(4):
        for c in range(4):
            line = [[field[at(a, b, c, h), :] for b in range(4)] for h in range(2)]
            normal = [combine(STIFF[3], line[h]) for h in range(2)]
            up = choose(
                ey, [subs(normal[1], -3), subs(normal[0], -2), subs(line[1][3], -1), line[0][3]]
            )
            normal = [combine(STIFF[0], line[h]) for h in range(2)]
            down = choose(
                ey, [line[0][0], subs(line[1][0], 1), subs(normal[0], 2), subs(normal[1], 3)]
            )
            give(near, far, (a * 4 + c) * ROWS, even, up, down)
    edge = [normals[pl.ds((12 + c) * ROWS, ROWS), :] for c in range(4)]
    up = choose(ey, [subs(edge[3], -3), subs(edge[2], -2), subs(edge[1], -1), edge[0]])
    edge = [normals[pl.ds(c * ROWS, ROWS), :] for c in range(4)]
    down = choose(ey, [edge[0], subs(edge[1], 1), subs(edge[2], 2), subs(edge[3], 3)])
    give(near, far, 16 * ROWS, even, up, down)


def image_kernel(
    len_axial, len_azim, len_radial, part, normals_in, near, far, field, image, sums, normals, sides
):
    lane, sub = iotas()
    top = sub < 4
    ey = sub & 3
    slab = lax.axis_index("stream")
    first = jnp.where(slab == 0, F32(0.0), F32(1.0))
    last = jnp.where(slab == lax.axis_size("stream") - 1, F32(0.0), F32(1.0))
    even = lax.rem(lax.axis_index("azim"), 2) == 0
    for a in range(4):
        for c in range(4):
            under, over = take(near, far, (a * 4 + c) * ROWS, even)
            under_face = [subs(under, -3), subs(under, -2)]
            under_normal = [subs(under, -1), under]
            over_face = [subs(over, 3), subs(over, 2)]
            over_normal = [subs(over, 1), over]
            for h in range(2):
                low = part[at(a, 0, c, h), :]
                high = part[at(a, 3, c, h), :]
                sides[pl.ds(((a * 4 + c) * 2 + h) * ROWS, ROWS), :] = jnp.where(
                    ey == 0,
                    under_normal[h] + float(STIFF[3, 3]) * low,
                    over_normal[h] + float(STIFF[0, 0]) * high,
                )
                field[at(a, 0, c, h), :] = low + jnp.where(ey == 0, under_face[h], 0.0)
                field[at(a, 3, c, h), :] = high + jnp.where(ey == 3, over_face[h], 0.0)
                for b in (1, 2):
                    field[at(a, b, c, h), :] = part[at(a, b, c, h), :]
    under, over = take(near, far, 16 * ROWS, even)
    for c in range(4):
        spot = pl.ds(c * ROWS, ROWS)
        normals[spot, :] = normals_in[spot, :] + jnp.where(ey == 0, subs(under, c - 3), 0.0)
        spot = pl.ds((12 + c) * ROWS, ROWS)
        normals[spot, :] = normals_in[spot, :] + jnp.where(ey == 3, subs(over, 3 - c), 0.0)
        for b in (1, 2):
            spot = pl.ds((b * 4 + c) * ROWS, ROWS)
            normals[spot, :] = normals_in[spot, :]

    axial, azim, radial, (before, after, beneath, beyond) = lengths(
        len_axial, len_azim, len_radial, sub
    )
    zero = jnp.zeros((ROWS, 128), F32)
    rx = [2.0 / axial[h] for h in range(2)]
    ry = 2.0 / azim
    rz = 2.0 / radial
    qz = 0.5 * radial
    qx = [[0.5 * axial[h] for a in range(4)] for h in range(2)]
    before_v, after_v = jnp.full((ROWS, 128), before, F32), jnp.full((ROWS, 128), after, F32)
    beneath_v, beyond_v = jnp.full((ROWS, 128), beneath, F32), jnp.full((ROWS, 128), beyond, F32)
    own_x = [qx[h][0] for h in range(2)]
    qx[0][0] = own_x[0] + jnp.where(top, first * 0.5 * before_v, 0.0)
    qx[1][3] = own_x[1] + jnp.where(top, 0.0, last * 0.5 * after_v)
    ghost_x = [jnp.where(top, first * 2.0 / before_v, 0.0), jnp.where(top, 0.0, last * 2.0 / after_v)]
    own_y = 0.5 * azim
    qy = [
        own_y + jnp.where(ey == 0, 0.5 * beneath_v, 0.0),
        own_y,
        own_y,
        own_y + jnp.where(ey == 3, 0.5 * beyond_v, 0.0),
    ]
    ghost_y = [jnp.where(ey == 0, 2.0 / beneath_v, 0.0), zero, zero, jnp.where(ey == 3, 2.0 / beyond_v, 0.0)]

    for h in range(2):
        factor = [rx[h] * qz * qy[b] for b in range(4)]
        extra = [ghost_x[h] * qz * qy[b] for b in range(4)]
        edge_a = 0 if h == 0 else 3
        for b in range(4):
            for c in range(4):
                line = [field[at(a, b, c, h), :] for a in range(4)]
                for a, value in enumerate(stiff_along(line)):
                    value = factor[b] * value
                    if a == edge_a:
                        value = value + extra[b] * normals[pl.ds((b * 4 + c) * ROWS, ROWS), :]
                    image[at(a, b, c, h), :] = float(WEIGHT[b] * WEIGHT[c]) * value
        for a in range(4):
            factor_a = ry * qz * qx[h][a]
            extra_a = [ghost_y[b] * qz * qx[h][a] for b in range(4)]
            for c in range(4):
                line = [field[at(a, b, c, h), :] for b in range(4)]
                side = sides[pl.ds(((a * 4 + c) * 2 + h) * ROWS, ROWS), :]
                for b, value in enumerate(stiff_along(line)):
                    value = factor_a * value
                    if b in (0, 3):
                        value = value + extra_a[b] * side
                    image[at(a, b, c, h), :] += float(WEIGHT[a] * WEIGHT[c]) * value
        for a in range(4):
            for b in range(4):
                factor_ab = (float(WEIGHT[a] * WEIGHT[b]) * rz) * qx[h][a] * qy[b]
                line = [field[at(a, b, c, h), :] for c in range(4)]
                line = [
                    image[at(a, b, c, h), :] + factor_ab * value
                    for c, value in enumerate(stiff_along(line))
                ]
                for c, value in enumerate(join_radial(line, lane)):
                    image[at(a, b, c, h), :] = value
    join_azim(image, sub)
    outlet = jnp.where(top, 1.0, last)
    for b in range(4):
        for c in range(4):
            low, high = join_axial(image, b, c, sub)
            high[1] = high[1] * outlet
            for h in range(2):
                image[at(0, b, c, h), :] = low[h]
                image[at(3, b, c, h), :] = high[h]

    load_load = load_image = image_image = zero
    for h in range(2):
        for a in range(3):
            for b in range(3):
                for c in range(3):
                    one, two = field[at(a, b, c, h), :], image[at(a, b, c, h), :]
                    load_load = load_load + one * one
                    load_image = load_image + one * two
                    image_image = image_image + two * two
    energy = zero
    for h in range(2):
        along = [zero, zero, zero]
        for m in range(4):
            for n in range(4):
                weight = float(WEIGHT[m] * WEIGHT[n])
                lines = (
                    [image[at(k, m, n, h), :] for k in range(4)],
                    [image[at(m, k, n, h), :] for k in range(4)],
                    [image[at(m, n, k, h), :] for k in range(4)],
                )
                for axis, line in enumerate(lines):
                    dot = None
                    for one, two in zip(line, stiff_along(line)):
                        term = one * two
                        dot = term if dot is None else dot + term
                    along[axis] = along[axis] + weight * dot
        energy = (
            energy
            + rx[h] * own_y * qz * along[0]
            + ry * own_x[h] * qz * along[1]
            + rz * own_x[h] * own_y * along[2]
        )
    row = zero
    for k, value in enumerate((load_load, load_image, image_image, energy)):
        value = jnp.sum(jnp.sum(value, axis=0, keepdims=True), axis=1, keepdims=True)
        row = jnp.where(lane == k, jnp.broadcast_to(value, (ROWS, 128)), row)
    for k in range(sums.shape[0] // ROWS):
        sums[pl.ds(k * ROWS, ROWS), :] = row


def final_kernel(
    len_axial, len_azim, len_radial, sums, field, image, pred, velocity_h, pressure_h, velocity, pressure, sems
):
    lane, sub = iotas()
    total = sums[pl.ds(0, ROWS), :]
    for k in range(1, sums.shape[0] // ROWS):
        total = total + sums[pl.ds(k * ROWS, ROWS), :]
    total = jnp.broadcast_to(jnp.sum(total, axis=0, keepdims=True), (ROWS, 128))
    s0, s1, s2, s3 = (
        jnp.broadcast_to(
            jnp.sum(jnp.where(lane == k, total, 0.0), axis=1, keepdims=True), (ROWS, 128)
        )
        for k in range(4)
    )
    alpha = s0 / s1
    ratio = s2 / s1
    grown = alpha * ratio
    energy = alpha * (s3 - s2 * ratio)
    second = s0 * (grown - 1.0) / (alpha * energy)
    of_load = alpha + second * grown
    of_image = -(second * alpha)

    axial, azim, radial, _ = lengths(len_axial, len_azim, len_radial, sub)
    for h in range(2):
        for a in range(4):
            for b in range(4):
                for c in range(4):
                    spot = at(a, b, c, h)
                    pressure[spot, :] = of_load * field[spot, :] + of_image * image[spot, :]
    leaving = [pltpu.make_async_copy(pressure, pressure_h, sems.at[9])]
    leaving[0].start()
    scales = [[2.0 / (axial[h], azim, radial)[axis] for h in range(2)] for axis in range(3)]

    def write(axis, line, h):
        values = slope_along([pressure[at(*node, h), :] for node in line])
        for (a, b, c), value in zip(line, values):
            spot = pl.ds(axis * 1024 + (a * 16 + b * 4 + c) * 16 + h * ROWS, ROWS)
            velocity[spot, :] = pred[spot, :] - scales[axis][h] * value

    def leave(first, rows):
        span = pl.ds(first, rows)
        leaving.append(
            pltpu.make_async_copy(velocity.at[span, :], velocity_h.at[span, :], sems.at[len(leaving) - 1])
        )
        leaving[-1].start()

    for m in range(4):
        for n in range(4):
            for h in range(2):
                write(0, [(k, m, n) for k in range(4)], h)
    leave(0, 1024)
    for axis in (1, 2):
        for a in range(4):
            for n in range(4):
                for h in range(2):
                    write(axis, [(a, k, n) if axis == 1 else (a, n, k) for k in range(4)], h)
            leave(axis * 1024 + a * 256, 256)
    for copy in leaving:
        copy.wait()


SMEM = pl.BlockSpec(memory_space=pltpu.SMEM)
VMEM = pl.BlockSpec(memory_space=pltpu.VMEM)
HBM = pl.BlockSpec(memory_space=pltpu.HBM)


def array(rows, kind=F32):
    return jax.ShapeDtypeStruct((rows, 128), kind)


def call(kernel, ins, outs, scratch, name, place=VMEM, limit=VMEM_LIMIT):
    return pl.pallas_call(
        kernel,
        out_shape=outs,
        in_specs=ins,
        out_specs=[place] * len(outs),
        scratch_shapes=scratch,
        compiler_params=pltpu.CompilerParams(vmem_limit_bytes=limit),
        name=name,
    )


def swapped(axis, near, far, closed):
    count = lax.axis_size(axis)
    apart = [(i + 1) % count if i % 2 else (i - 1) % count for i in range(count)]
    if not closed:
        apart[0], apart[-1] = 0, count - 1
    far = lax.ppermute(far, axis, list(enumerate(apart)))
    return lax.ppermute(near, axis, [(i, i ^ 1) for i in range(count)]), far


def body(history, block_ids, len_axial, len_azim, len_radial, solid):
    slabs, sectors = lax.axis_size("stream"), lax.axis_size("azim")
    radial = len_radial.reshape(1, 128)
    geometry = (len_axial, len_azim, radial)
    geometry_specs = [SMEM, SMEM, VMEM]
    hist = history.reshape(576, history.shape[3])
    send, keep = call(
        pack_kernel,
        [HBM] * 5,
        [array(slabs * PEER_ROWS), array(128 * BLOCK_ROWS)],
        [
            pltpu.VMEM(hist.shape, F32),
            pltpu.VMEM((slabs * PEER_ROWS, 128), F32),
            pltpu.VMEM((128 * BLOCK_ROWS, 128), F32),
            pltpu.SMEM(block_ids.shape, jnp.int32),
            pltpu.SMEM(len_axial.shape, F32),
            pltpu.SMEM(len_azim.shape, F32),
            pltpu.VMEM((1, 128), F32),
            pltpu.SMEM((slabs,), jnp.int32),
            pltpu.SMEM((CAP * slabs + 1,), jnp.int32),
            pltpu.VMEM((ROWS, 128), F32),
            pltpu.SemaphoreType.DMA((CHUNKS,)),
            pltpu.SemaphoreType.DMA((CHUNKS,)),
            pltpu.SemaphoreType.DMA((4,)),
        ],
        "pack",
        HBM,
        limit=PACK_LIMIT,
    )(block_ids, *geometry, hist)
    arrived = lax.all_to_all(
        send.reshape(slabs, PEER_ROWS, 128), "stream", split_axis=0, concat_axis=0, tiled=True
    ).reshape(slabs * PEER_ROWS, 128)
    pred, part, near, far = call(
        load_kernel,
        [SMEM] + geometry_specs + [VMEM] * 3,
        [array(3 * 1024), array(1024), array(128), array(128)],
        [
            pltpu.VMEM((ROWS, 128), jnp.int32),
            pltpu.SMEM((ROWS, 128), jnp.int32),
            pltpu.SMEM((129,), jnp.int32),
            pltpu.SemaphoreType.DMA(()),
        ],
        "load",
    )(block_ids, *geometry, solid.reshape(16, 128), arrived, keep)
    near, far = swapped("stream", near, far, False)
    part, normals, near, far = call(
        axial_kernel,
        [VMEM] * 3,
        [array(1024), array(128), array(136), array(136)],
        [],
        "axial_faces",
    )(part, near, far)
    near, far = swapped("azim", near, far, True)
    field, image, sums = call(
        image_kernel,
        geometry_specs + [VMEM] * 4,
        [array(1024), array(1024), array(slabs * sectors)],
        [pltpu.VMEM((128, 128), F32), pltpu.VMEM((256, 128), F32)],
        "image",
    )(*geometry, part, normals, near, far)
    sums = lax.all_to_all(
        sums.reshape(slabs * sectors, 1, 128),
        ("stream", "azim"),
        split_axis=0,
        concat_axis=0,
        tiled=True,
    ).reshape(slabs * sectors, 128)
    velocity, pressure = call(
        final_kernel,
        geometry_specs + [VMEM] * 4,
        [array(3 * 1024), array(1024)],
        [
            pltpu.VMEM((3 * 1024, 128), F32),
            pltpu.VMEM((1024, 128), F32),
            pltpu.SemaphoreType.DMA((10,)),
        ],
        "velocity",
        HBM,
    )(*geometry, sums, field, image, pred)
    return velocity.reshape(3, 4, 4, 4, 4, 4, 128), pressure.reshape(4, 4, 4, 4, 4, 128)


def solution(mesh):
    in_specs = (
        P(None, None, None, ("stream", "azim")),
        P(("stream", "azim")),
        P(),
        P(),
        P(),
        P("stream", "azim", None),
    )
    out_specs = (
        P(None, None, None, None, "stream", "azim", None),
        P(None, None, None, "stream", "azim", None),
    )
    return jax.shard_map(body, mesh=mesh, in_specs=in_specs, out_specs=out_specs, check_vma=False)
```

```python
import functools
import math

import jax
import jax.numpy as jnp
import numpy as np
from jax import lax
from jax.experimental import pallas as pl
from jax.experimental.pallas import tpu as pltpu
from jax.sharding import PartitionSpec as P

CAP = 2
DT = 0.01
PENALTY = 100.0
VMEM_LIMIT = 40 * 1024 * 1024
PACK_LIMIT = 60 * 1024 * 1024
F32 = jnp.float32


def node_tables():
    root = 1.0 / math.sqrt(5.0)
    points = np.array([-1.0, -root, root, 1.0])
    weights = np.array([1.0 / 6.0, 5.0 / 6.0, 5.0 / 6.0, 1.0 / 6.0])
    legendre = (5.0 * points**3 - 3.0 * points) / 2.0
    slope = np.zeros((4, 4))
    for first in range(4):
        for second in range(4):
            if first != second:
                slope[first, second] = legendre[first] / (
                    legendre[second] * (points[first] - points[second])
                )
    slope[0, 0] = -3.0
    slope[3, 3] = 3.0
    return slope, weights


SLOPE, WEIGHT = node_tables()
STIFF = SLOPE.T @ np.diag(WEIGHT) @ SLOPE
EDGE = float(WEIGHT[0])

ROWS = 8
BLOCK_ROWS = 24
PEER_ROWS = CAP * BLOCK_ROWS + ROWS


def iotas():
    lane = lax.broadcasted_iota(jnp.int32, (ROWS, 128), 1)
    sub = lax.broadcasted_iota(jnp.int32, (ROWS, 128), 0)
    return lane, sub


def lanes(x, shift):
    shift %= 128
    return pltpu.roll(x, shift, 1) if shift else x


def subs(x, shift):
    shift %= ROWS
    return pltpu.roll(x, shift, 0) if shift else x


def combine(coefs, values, factor=1.0):
    total = None
    for coef, value in zip(coefs, values):
        coef = factor * float(coef)
        term = coef * value
        total = term if total is None else total + term
    return total


def halves(line):
    return (line[0] + line[3], line[1] + line[2]), (line[0] - line[3], line[1] - line[2])


def slope_along(line):
    even, odd = halves(line)
    first = [combine(SLOPE[i, :2] - SLOPE[i, :1:-1], odd, 0.5) for i in range(2)]
    second = [combine(SLOPE[i, :2] + SLOPE[i, :1:-1], even, 0.5) for i in range(2)]
    return [first[0] + second[0], first[1] + second[1], first[1] - second[1], first[0] - second[0]]


def stiff_along(line):
    even, odd = halves(line)
    first = [combine(STIFF[i, :2] + STIFF[i, :1:-1], even, 0.5) for i in range(2)]
    second = [combine(STIFF[i, :2] - STIFF[i, :1:-1], odd, 0.5) for i in range(2)]
    return [first[0] + second[0], first[1] + second[1], first[1] - second[1], first[0] - second[0]]


def choose(key, values):
    result = values[0]
    for at in range(1, len(values)):
        result = jnp.where(key == at, values[at], result)
    return result


def swap_groups(tiles, group):
    mixed = [lanes(tile, 16 * t) for t, tile in enumerate(tiles)]
    for bit in (1, 2, 4):
        odd = (group & bit) != 0
        mixed = [jnp.where(odd, mixed[(t + bit) & 7], mixed[t]) for t in range(8)]
    return [lanes(mixed[-g & 7], -16 * g) for g in range(8)]


CHUNKS = 4


def pack_kernel(
    ids_h, axial_h, azim_h, radial_h, hist_h, send_h, keep_h,
    hist, send, keep, ids, len_axial, len_azim, len_radial, count, labels, table,
    hist_sem, keep_sem, small_sem,
):
    sectors = lax.axis_size("azim")
    peers = lax.axis_size("stream")
    me = lax.axis_index("stream")
    width = hist.shape[1] // CHUNKS
    columns = width // 128

    def chunk(n):
        span = pl.ds(pl.multiple_of(n * width, width), width)
        return pltpu.make_async_copy(hist_h.at[:, span], hist.at[:, span], hist_sem.at[n])

    def kept(n):
        rows = keep.shape[0] // CHUNKS
        span = pl.ds(pl.multiple_of(n * rows, rows), rows)
        return pltpu.make_async_copy(keep.at[span, :], keep_h.at[span, :], keep_sem.at[n])

    small = [
        pltpu.make_async_copy(source, target, small_sem.at[n])
        for n, (source, target) in enumerate(
            ((ids_h, ids), (axial_h, len_axial), (azim_h, len_azim), (radial_h, len_radial))
        )
    ]
    for copy in small:
        copy.start()
    for n in range(CHUNKS):
        chunk(n).start()
    lane, sub = iotas()
    group = lane >> 4
    c_at = sub & 3
    for t in range(peers):
        count[t] = 0
    for n in range(CAP * peers):
        labels[n] = 0
    for copy in small:
        copy.wait()
    whole = jnp.broadcast_to(len_radial[...], (ROWS, 128))
    rows = choose(sub, [lanes(whole, -16 * z) for z in range(8)])
    rows = jnp.where(group == 0, rows, 0.0)
    for shift in (16, 32, 64):
        rows = rows + lanes(rows, shift)
    table[...] = rows

    def pattern(low, high):
        return jnp.where(sub < 4, F32(low), F32(high))

    def column(at):
        offset = pl.multiple_of(at * 128, 128)

        def level(which, comp, t):
            return hist[pl.ds((which * 3 + comp) * 64 + 8 * t, ROWS), pl.ds(offset, 128)]

        places = []
        axial = azim = radial = None
        for piece in range(8):
            ident = ids[at * 8 + piece]
            owner = ident >> 7
            slot = ident & 127
            flow = owner // sectors
            sector = owner - flow * sectors
            moving = flow != me
            rank = jnp.where(moving, count[flow], 0)
            count[flow] = rank + 1
            labels[jnp.where(moving, flow * CAP + rank, CAP * peers)] = slot + 1
            places.append(
                (flow * PEER_ROWS + rank * BLOCK_ROWS, (at * 8 + piece) * BLOCK_ROWS)
            )
            one_axial = len_axial[flow * 4 + (slot >> 5)]
            one_azim = len_azim[sector * 4 + ((slot >> 3) & 3)]
            one_radial = table[pl.ds(slot & 7, 1), :]
            if piece == 0:
                axial = jnp.full((ROWS, 128), one_axial, F32)
                azim = jnp.full((ROWS, 128), one_azim, F32)
                radial = jnp.broadcast_to(one_radial, (ROWS, 128))
            else:
                axial = jnp.where(group == piece, one_axial, axial)
                azim = jnp.where(group == piece, one_azim, azim)
                radial = jnp.where(group == piece, one_radial, radial)
        scales = [(-2.0 * DT) / length for length in (axial, azim, radial)]

        extrap = [
            [3.0 * (level(0, comp, t) - level(1, comp, t)) + level(2, comp, t) for t in range(8)]
            for comp in range(3)
        ]
        wind = [[scales[axis] * extrap[axis][t] for t in range(8)] for axis in range(3)]
        spin = []
        for k in range(4):
            value = jnp.zeros((ROWS, 128), F32)
            for c in range(4):
                value = jnp.where(c_at == c, F32(SLOPE[c, (c + k) % 4]), value)
            spin.append(value)
        same = [[pattern(SLOPE[2 * p, 2 * o], SLOPE[2 * p + 1, 2 * o + 1]) for o in range(2)] for p in range(2)]
        cross = [[pattern(SLOPE[2 * p, 2 * o + 1], SLOPE[2 * p + 1, 2 * o]) for o in range(2)] for p in range(2)]
        for comp in range(3):
            ue = extrap[comp]
            flipped = [subs(ue[t], 4) for t in range(8)]
            along_a = [None] * 8
            for half in range(2):
                for a, value in enumerate(slope_along([ue[2 * o + half] for o in range(4)])):
                    along_a[2 * a + half] = value
            tiles = []
            for t in range(8):
                a, half = t // 2, t % 2
                along_b = (
                    same[half][0] * ue[2 * a]
                    + cross[half][0] * flipped[2 * a]
                    + same[half][1] * ue[2 * a + 1]
                    + cross[half][1] * flipped[2 * a + 1]
                )
                along_c = spin[0] * ue[t]
                for k in range(1, 4):
                    along_c = along_c + spin[k] * subs(jnp.where(c_at < k, flipped[t], ue[t]), -k)
                advect = wind[0][t] * along_a[t] + wind[1][t] * along_b + wind[2][t] * along_c
                base = ue[t] + 1.5 * level(1, comp, t) - F32(2.0 / 3.0) * level(2, comp, t)
                tiles.append(base + advect)
            for (to_send, to_keep), tile in zip(places, swap_groups(tiles, group)):
                send[pl.ds(pl.multiple_of(to_send + comp * ROWS, ROWS), ROWS), :] = tile
                keep[pl.ds(pl.multiple_of(to_keep + comp * ROWS, ROWS), ROWS), :] = tile

    @pl.loop(0, CHUNKS)
    def _(n):
        chunk(n).wait()
        for k in range(columns):
            column(n * columns + k)
        kept(n).start()

    corner = sub == 0
    for t in range(peers):
        marks = jnp.zeros((ROWS, 128), jnp.int32)
        for rank in range(CAP):
            marks = jnp.where(corner & (lane == CAP * me + rank), labels[t * CAP + rank], marks)
        send[pl.ds(t * PEER_ROWS + CAP * BLOCK_ROWS, ROWS), :] = marks.astype(F32)
    leaving = pltpu.make_async_copy(send, send_h, small_sem.at[0])
    leaving.start()
    for n in range(CHUNKS):
        kept(n).wait()
    leaving.wait()


def at(a, b, c, h):
    return pl.ds((a * 16 + b * 4 + c) * 16 + h * ROWS, ROWS)


def join_radial(line, lane):
    first = line[0] + jnp.where(lane == 0, 0.0, lanes(line[3], 1))
    last = jnp.where(lane == 127, 0.0, lanes(first, -1))
    return [first, line[1], line[2], last]


def join_azim(ref, sub):
    ey = sub & 3
    for a in range(4):
        for c in range(4):
            for h in range(2):
                low = ref[at(a, 0, c, h), :]
                high = ref[at(a, 3, c, h), :]
                ref[at(a, 0, c, h), :] = low + jnp.where(ey == 0, 0.0, subs(high, 1))
                ref[at(a, 3, c, h), :] = high + jnp.where(ey == 3, 0.0, subs(low, -1))


def join_axial(ref, b, c, sub):
    top = sub < 4
    low = [ref[at(0, b, c, h), :] for h in range(2)]
    high = [ref[at(3, b, c, h), :] for h in range(2)]
    low_turned = [subs(x, 4) for x in low]
    high_turned = [subs(x, 4) for x in high]
    new_low = [
        low[0] + jnp.where(top, 0.0, high_turned[0]),
        low[1] + jnp.where(top, high_turned[0], high_turned[1]),
    ]
    new_high = [
        high[0] + jnp.where(top, low_turned[0], low_turned[1]),
        high[1] + jnp.where(top, low_turned[1], 0.0),
    ]
    return new_low, new_high


def lengths(len_axial, len_azim, len_radial, sub):
    slab = lax.axis_index("stream")
    sector = lax.axis_index("azim")
    columns, rows = len_axial.shape[0], len_azim.shape[0]
    x0, y0 = slab * 4, sector * 4
    top = sub < 4
    axial = [jnp.where(top, len_axial[x0 + 2 * h], len_axial[x0 + 2 * h + 1]) for h in range(2)]
    azim = choose(sub & 3, [jnp.full((ROWS, 128), len_azim[y0 + k], F32) for k in range(4)])
    radial = jnp.broadcast_to(len_radial[...], (ROWS, 128))
    before = len_axial[jnp.maximum(x0 - 1, 0)]
    after = len_axial[jnp.minimum(x0 + 4, columns - 1)]
    below = len_azim[lax.rem(y0 + rows - 1, rows)]
    above = len_azim[lax.rem(y0 + 4, rows)]
    return axial, azim, radial, (before, after, below, above)


def give(near, far, row, even, up, down):
    near[pl.ds(row, ROWS), :] = jnp.where(even, up, down)
    far[pl.ds(row, ROWS), :] = jnp.where(even, down, up)


def take(near, far, row, even):
    one, two = near[pl.ds(row, ROWS), :], far[pl.ds(row, ROWS), :]
    return jnp.where(even, two, one), jnp.where(even, one, two)


def load_kernel(
    ids, len_axial, len_azim, len_radial, solid, arrived, keep, pred, part, near, far,
    marks, marks_s, source, sem,
):
    lane, sub = iotas()
    group = lane >> 4
    peers = arrived.shape[0] // PEER_ROWS
    total = None
    for t in range(peers):
        tile = arrived[pl.ds(t * PEER_ROWS + CAP * BLOCK_ROWS, ROWS), :]
        total = tile if total is None else total + tile
    marks[...] = total.astype(jnp.int32)
    scalars = pltpu.make_async_copy(marks, marks_s, sem)
    scalars.start()
    slab, sectors = lax.axis_index("stream"), lax.axis_size("azim")
    for p in range(ids.shape[0]):
        ident = ids[p]
        stays = (ident >> 7) // sectors == slab
        source[jnp.where(stays, ident & 127, 128)] = -1 - p * BLOCK_ROWS
    scalars.wait()
    for n in range(peers * CAP):
        label = marks_s[0, n]
        source[jnp.where(label > 0, label - 1, 128)] = (
            (n // CAP) * PEER_ROWS + (n % CAP) * BLOCK_ROWS
        )

    def unpack(j, carry):
        places = [source[j * 8 + g] for g in range(8)]
        for comp in range(3):
            tiles = []
            for g, place in enumerate(places):
                row = pl.multiple_of(jnp.maximum(-1 - place, 0) + comp * ROWS, ROWS)
                kept = keep[pl.ds(row, ROWS), :]
                row = pl.multiple_of(jnp.maximum(place, 0) + comp * ROWS, ROWS)
                tiles.append(jnp.where(place >= 0, arrived[pl.ds(row, ROWS), :], kept))
            for t, tile in enumerate(swap_groups(tiles, group)):
                pred[pl.ds(comp * 1024 + 8 * t * 16 + j, ROWS, stride=16), :] = tile
        return carry

    lax.fori_loop(0, 16, unpack, 0, unroll=2)

    axial, azim, radial, _ = lengths(len_axial, len_azim, len_radial, sub)
    inverse = [
        1.0 / (F32(11.0 / 6.0) + F32(DT * PENALTY) * solid[pl.ds(h * ROWS, ROWS), :].astype(F32))
        for h in range(2)
    ]

    def scaled(comp, a, b, c, h):
        spot = pl.ds(comp * 1024 + (a * 16 + b * 4 + c) * 16 + h * ROWS, ROWS)
        value = pred[spot, :] * inverse[h]
        pred[spot, :] = value
        return value

    area = [
        [0.25 * azim * radial for h in range(2)],
        [0.25 * axial[h] * radial for h in range(2)],
        [0.25 * axial[h] * azim for h in range(2)],
    ]
    for h in range(2):
        for b in range(4):
            for c in range(4):
                line = [scaled(0, a, b, c, h) for a in range(4)]
                for a, value in enumerate(slope_along(line)):
                    part[at(a, b, c, h), :] = area[0][h] * value
        for a in range(4):
            for c in range(4):
                line = [scaled(1, a, b, c, h) for b in range(4)]
                for b, value in enumerate(slope_along(line)):
                    part[at(a, b, c, h), :] += area[1][h] * value
        for a in range(4):
            for b in range(4):
                line = [scaled(2, a, b, c, h) for c in range(4)]
                line = [
                    float(-WEIGHT[a] * WEIGHT[b] * WEIGHT[c])
                    * (part[at(a, b, c, h), :] + area[2][h] * value)
                    for c, value in enumerate(slope_along(line))
                ]
                for c, value in enumerate(join_radial(line, lane)):
                    part[at(a, b, c, h), :] = value
    join_azim(part, sub)
    top = sub < 4
    even = lax.rem(slab, 2) == 0
    for b in range(4):
        for c in range(4):
            low, high = join_axial(part, b, c, sub)
            for h in range(2):
                part[at(0, b, c, h), :] = low[h]
                part[at(3, b, c, h), :] = high[h]
            inner = [[part[at(a, b, c, h), :] for a in (1, 2)] for h in range(2)]
            normal = combine(STIFF[3], [low[1], *inner[1], high[1]])
            up = jnp.where(top, subs(high[1], 4), normal)
            normal = combine(STIFF[0], [low[0], *inner[0], high[0]])
            down = jnp.where(top, low[0], subs(normal, 4))
            give(near, far, (b * 4 + c) * ROWS, even, up, down)


def axial_kernel(part, near_in, far_in, field, normals, near, far):
    lane, sub = iotas()
    top = sub < 4
    slab = lax.axis_index("stream")
    first = jnp.where(slab == 0, F32(0.0), F32(1.0))
    last = jnp.where(slab == lax.axis_size("stream") - 1, F32(0.0), F32(1.0))
    even = lax.rem(slab, 2) == 0
    for b in range(4):
        for c in range(4):
            spot = pl.ds((b * 4 + c) * ROWS, ROWS)
            low = part[at(0, b, c, 0), :]
            high = part[at(3, b, c, 1), :]
            under, over = take(near_in, far_in, (b * 4 + c) * ROWS, even)
            normals[spot, :] = jnp.where(
                top,
                subs(under, 4) + float(STIFF[3, 3]) * low,
                over + float(STIFF[0, 0]) * high,
            )
            field[at(0, b, c, 0), :] = low + jnp.where(top, first * under, 0.0)
            field[at(3, b, c, 1), :] = jnp.where(top, high, last * (high + subs(over, 4)))
            field[at(0, b, c, 1), :] = part[at(0, b, c, 1), :]
            field[at(3, b, c, 0), :] = part[at(3, b, c, 0), :]
            for a in (1, 2):
                for h in range(2):
                    field[at(a, b, c, h), :] = part[at(a, b, c, h), :]
    ey = sub & 3
    even = lax.rem(lax.axis_index("azim"), 2) == 0
    for a in range(4):
        for c in range(4):
            line = [[field[at(a, b, c, h), :] for b in range(4)] for h in range(2)]
            normal = [combine(STIFF[3], line[h]) for h in range(2)]
            up = choose(
                ey, [subs(normal[1], -3), subs(normal[0], -2), subs(line[1][3], -1), line[0][3]]
            )
            normal = [combine(STIFF[0], line[h]) for h in range(2)]
            down = choose(
                ey, [line[0][0], subs(line[1][0], 1), subs(normal[0], 2), subs(normal[1], 3)]
            )
            give(near, far, (a * 4 + c) * ROWS, even, up, down)
    edge = [normals[pl.ds((12 + c) * ROWS, ROWS), :] for c in range(4)]
    up = choose(ey, [subs(edge[3], -3), subs(edge[2], -2), subs(edge[1], -1), edge[0]])
    edge = [normals[pl.ds(c * ROWS, ROWS), :] for c in range(4)]
    down = choose(ey, [edge[0], subs(edge[1], 1), subs(edge[2], 2), subs(edge[3], 3)])
    give(near, far, 16 * ROWS, even, up, down)


def image_kernel(
    len_axial, len_azim, len_radial, part, normals_in, near, far, field, image, sums, normals, sides
):
    lane, sub = iotas()
    top = sub < 4
    ey = sub & 3
    slab = lax.axis_index("stream")
    first = jnp.where(slab == 0, F32(0.0), F32(1.0))
    last = jnp.where(slab == lax.axis_size("stream") - 1, F32(0.0), F32(1.0))
    even = lax.rem(lax.axis_index("azim"), 2) == 0
    for a in range(4):
        for c in range(4):
            under, over = take(near, far, (a * 4 + c) * ROWS, even)
            under_face = [subs(under, -3), subs(under, -2)]
            under_normal = [subs(under, -1), under]
            over_face = [subs(over, 3), subs(over, 2)]
            over_normal = [subs(over, 1), over]
            for h in range(2):
                low = part[at(a, 0, c, h), :]
                high = part[at(a, 3, c, h), :]
                sides[pl.ds(((a * 4 + c) * 2 + h) * ROWS, ROWS), :] = jnp.where(
                    ey == 0,
                    under_normal[h] + float(STIFF[3, 3]) * low,
                    over_normal[h] + float(STIFF[0, 0]) * high,
                )
                field[at(a, 0, c, h), :] = low + jnp.where(ey == 0, under_face[h], 0.0)
                field[at(a, 3, c, h), :] = high + jnp.where(ey == 3, over_face[h], 0.0)
                for b in (1, 2):
                    field[at(a, b, c, h), :] = part[at(a, b, c, h), :]
    under, over = take(near, far, 16 * ROWS, even)
    for c in range(4):
        spot = pl.ds(c * ROWS, ROWS)
        normals[spot, :] = normals_in[spot, :] + jnp.where(ey == 0, subs(under, c - 3), 0.0)
        spot = pl.ds((12 + c) * ROWS, ROWS)
        normals[spot, :] = normals_in[spot, :] + jnp.where(ey == 3, subs(over, 3 - c), 0.0)
        for b in (1, 2):
            spot = pl.ds((b * 4 + c) * ROWS, ROWS)
            normals[spot, :] = normals_in[spot, :]

    axial, azim, radial, (before, after, beneath, beyond) = lengths(
        len_axial, len_azim, len_radial, sub
    )
    zero = jnp.zeros((ROWS, 128), F32)
    rx = [2.0 / axial[h] for h in range(2)]
    ry = 2.0 / azim
    rz = 2.0 / radial
    qz = 0.5 * radial
    qx = [[0.5 * axial[h] for a in range(4)] for h in range(2)]
    before_v, after_v = jnp.full((ROWS, 128), before, F32), jnp.full((ROWS, 128), after, F32)
    beneath_v, beyond_v = jnp.full((ROWS, 128), beneath, F32), jnp.full((ROWS, 128), beyond, F32)
    own_x = [qx[h][0] for h in range(2)]
    qx[0][0] = own_x[0] + jnp.where(top, first * 0.5 * before_v, 0.0)
    qx[1][3] = own_x[1] + jnp.where(top, 0.0, last * 0.5 * after_v)
    ghost_x = [jnp.where(top, first * 2.0 / before_v, 0.0), jnp.where(top, 0.0, last * 2.0 / after_v)]
    own_y = 0.5 * azim
    qy = [
        own_y + jnp.where(ey == 0, 0.5 * beneath_v, 0.0),
        own_y,
        own_y,
        own_y + jnp.where(ey == 3, 0.5 * beyond_v, 0.0),
    ]
    ghost_y = [jnp.where(ey == 0, 2.0 / beneath_v, 0.0), zero, zero, jnp.where(ey == 3, 2.0 / beyond_v, 0.0)]

    for h in range(2):
        factor = [rx[h] * qz * qy[b] for b in range(4)]
        extra = [ghost_x[h] * qz * qy[b] for b in range(4)]
        edge_a = 0 if h == 0 else 3
        for b in range(4):
            for c in range(4):
                line = [field[at(a, b, c, h), :] for a in range(4)]
                for a, value in enumerate(stiff_along(line)):
                    value = factor[b] * value
                    if a == edge_a:
                        value = value + extra[b] * normals[pl.ds((b * 4 + c) * ROWS, ROWS), :]
                    image[at(a, b, c, h), :] = float(WEIGHT[b] * WEIGHT[c]) * value
        for a in range(4):
            factor_a = ry * qz * qx[h][a]
            extra_a = [ghost_y[b] * qz * qx[h][a] for b in range(4)]
            for c in range(4):
                line = [field[at(a, b, c, h), :] for b in range(4)]
                side = sides[pl.ds(((a * 4 + c) * 2 + h) * ROWS, ROWS), :]
                for b, value in enumerate(stiff_along(line)):
                    value = factor_a * value
                    if b in (0, 3):
                        value = value + extra_a[b] * side
                    image[at(a, b, c, h), :] += float(WEIGHT[a] * WEIGHT[c]) * value
        for a in range(4):
            for b in range(4):
                factor_ab = (float(WEIGHT[a] * WEIGHT[b]) * rz) * qx[h][a] * qy[b]
                line = [field[at(a, b, c, h), :] for c in range(4)]
                line = [
                    image[at(a, b, c, h), :] + factor_ab * value
                    for c, value in enumerate(stiff_along(line))
                ]
                for c, value in enumerate(join_radial(line, lane)):
                    image[at(a, b, c, h), :] = value
    join_azim(image, sub)
    outlet = jnp.where(top, 1.0, last)
    for b in range(4):
        for c in range(4):
            low, high = join_axial(image, b, c, sub)
            high[1] = high[1] * outlet
            for h in range(2):
                image[at(0, b, c, h), :] = low[h]
                image[at(3, b, c, h), :] = high[h]

    load_load = load_image = image_image = zero
    for h in range(2):
        for a in range(3):
            for b in range(3):
                for c in range(3):
                    one, two = field[at(a, b, c, h), :], image[at(a, b, c, h), :]
                    load_load = load_load + one * one
                    load_image = load_image + one * two
                    image_image = image_image + two * two
    energy = zero
    for h in range(2):
        along = [zero, zero, zero]
        for m in range(4):
            for n in range(4):
                weight = float(WEIGHT[m] * WEIGHT[n])
                lines = (
                    [image[at(k, m, n, h), :] for k in range(4)],
                    [image[at(m, k, n, h), :] for k in range(4)],
                    [image[at(m, n, k, h), :] for k in range(4)],
                )
                for axis, line in enumerate(lines):
                    dot = None
                    for one, two in zip(line, stiff_along(line)):
                        term = one * two
                        dot = term if dot is None else dot + term
                    along[axis] = along[axis] + weight * dot
        energy = (
            energy
            + rx[h] * own_y * qz * along[0]
            + ry * own_x[h] * qz * along[1]
            + rz * own_x[h] * own_y * along[2]
        )
    row = zero
    for k, value in enumerate((load_load, load_image, image_image, energy)):
        value = jnp.sum(jnp.sum(value, axis=0, keepdims=True), axis=1, keepdims=True)
        row = jnp.where(lane == k, jnp.broadcast_to(value, (ROWS, 128)), row)
    for k in range(sums.shape[0] // ROWS):
        sums[pl.ds(k * ROWS, ROWS), :] = row


def final_kernel(
    len_axial, len_azim, len_radial, sums, field, image, pred, velocity_h, pressure_h, velocity, pressure, sems
):
    lane, sub = iotas()
    total = sums[pl.ds(0, ROWS), :]
    for k in range(1, sums.shape[0] // ROWS):
        total = total + sums[pl.ds(k * ROWS, ROWS), :]
    total = jnp.broadcast_to(jnp.sum(total, axis=0, keepdims=True), (ROWS, 128))
    s0, s1, s2, s3 = (
        jnp.broadcast_to(
            jnp.sum(jnp.where(lane == k, total, 0.0), axis=1, keepdims=True), (ROWS, 128)
        )
        for k in range(4)
    )
    alpha = s0 / s1
    ratio = s2 / s1
    grown = alpha * ratio
    energy = alpha * (s3 - s2 * ratio)
    second = s0 * (grown - 1.0) / (alpha * energy)
    of_load = alpha + second * grown
    of_image = -(second * alpha)

    axial, azim, radial, _ = lengths(len_axial, len_azim, len_radial, sub)
    for h in range(2):
        for a in range(4):
            for b in range(4):
                for c in range(4):
                    spot = at(a, b, c, h)
                    pressure[spot, :] = of_load * field[spot, :] + of_image * image[spot, :]
    leaving = [pltpu.make_async_copy(pressure, pressure_h, sems.at[3])]
    leaving[0].start()
    for axis in range(3):
        for h in range(2):
            scale = 2.0 / (axial[h], azim, radial)[axis]
            for m in range(4):
                for n in range(4):
                    line = [(k, m, n) if axis == 0 else (m, k, n) if axis == 1 else (m, n, k) for k in range(4)]
                    values = slope_along([pressure[at(*node, h), :] for node in line])
                    for (a, b, c), value in zip(line, values):
                        spot = pl.ds(axis * 1024 + (a * 16 + b * 4 + c) * 16 + h * ROWS, ROWS)
                        velocity[spot, :] = pred[spot, :] - scale * value
        span = pl.ds(axis * 1024, 1024)
        leaving.append(pltpu.make_async_copy(velocity.at[span, :], velocity_h.at[span, :], sems.at[axis]))
        leaving[-1].start()
    for copy in leaving:
        copy.wait()


SMEM = pl.BlockSpec(memory_space=pltpu.SMEM)
VMEM = pl.BlockSpec(memory_space=pltpu.VMEM)
HBM = pl.BlockSpec(memory_space=pltpu.HBM)


def array(rows, kind=F32):
    return jax.ShapeDtypeStruct((rows, 128), kind)


def call(kernel, ins, outs, scratch, name, place=VMEM, limit=VMEM_LIMIT):
    return pl.pallas_call(
        kernel,
        out_shape=outs,
        in_specs=ins,
        out_specs=[place] * len(outs),
        scratch_shapes=scratch,
        compiler_params=pltpu.CompilerParams(vmem_limit_bytes=limit),
        name=name,
    )


def swapped(axis, near, far, closed):
    count = lax.axis_size(axis)
    apart = [(i + 1) % count if i % 2 else (i - 1) % count for i in range(count)]
    if not closed:
        apart[0], apart[-1] = 0, count - 1
    far = lax.ppermute(far, axis, list(enumerate(apart)))
    return lax.ppermute(near, axis, [(i, i ^ 1) for i in range(count)]), far


def body(history, block_ids, len_axial, len_azim, len_radial, solid):
    slabs, sectors = lax.axis_size("stream"), lax.axis_size("azim")
    radial = len_radial.reshape(1, 128)
    geometry = (len_axial, len_azim, radial)
    geometry_specs = [SMEM, SMEM, VMEM]
    hist = history.reshape(576, history.shape[3])
    send, keep = call(
        pack_kernel,
        [HBM] * 5,
        [array(slabs * PEER_ROWS), array(128 * BLOCK_ROWS)],
        [
            pltpu.VMEM(hist.shape, F32),
            pltpu.VMEM((slabs * PEER_ROWS, 128), F32),
            pltpu.VMEM((128 * BLOCK_ROWS, 128), F32),
            pltpu.SMEM(block_ids.shape, jnp.int32),
            pltpu.SMEM(len_axial.shape, F32),
            pltpu.SMEM(len_azim.shape, F32),
            pltpu.VMEM((1, 128), F32),
            pltpu.SMEM((slabs,), jnp.int32),
            pltpu.SMEM((CAP * slabs + 1,), jnp.int32),
            pltpu.VMEM((ROWS, 128), F32),
            pltpu.SemaphoreType.DMA((CHUNKS,)),
            pltpu.SemaphoreType.DMA((CHUNKS,)),
            pltpu.SemaphoreType.DMA((4,)),
        ],
        "pack",
        HBM,
        limit=PACK_LIMIT,
    )(block_ids, *geometry, hist)
    arrived = lax.all_to_all(
        send.reshape(slabs, PEER_ROWS, 128), "stream", split_axis=0, concat_axis=0, tiled=True
    ).reshape(slabs * PEER_ROWS, 128)
    pred, part, near, far = call(
        load_kernel,
        [SMEM] + geometry_specs + [VMEM] * 3,
        [array(3 * 1024), array(1024), array(128), array(128)],
        [
            pltpu.VMEM((ROWS, 128), jnp.int32),
            pltpu.SMEM((ROWS, 128), jnp.int32),
            pltpu.SMEM((129,), jnp.int32),
            pltpu.SemaphoreType.DMA(()),
        ],
        "load",
    )(block_ids, *geometry, solid.reshape(16, 128), arrived, keep)
    near, far = swapped("stream", near, far, False)
    part, normals, near, far = call(
        axial_kernel,
        [VMEM] * 3,
        [array(1024), array(128), array(136), array(136)],
        [],
        "axial_faces",
    )(part, near, far)
    near, far = swapped("azim", near, far, True)
    field, image, sums = call(
        image_kernel,
        geometry_specs + [VMEM] * 4,
        [array(1024), array(1024), array(slabs * sectors)],
        [pltpu.VMEM((128, 128), F32), pltpu.VMEM((256, 128), F32)],
        "image",
    )(*geometry, part, normals, near, far)
    sums = lax.all_to_all(
        sums.reshape(slabs * sectors, 1, 128),
        ("stream", "azim"),
        split_axis=0,
        concat_axis=0,
        tiled=True,
    ).reshape(slabs * sectors, 128)
    velocity, pressure = call(
        final_kernel,
        geometry_specs + [VMEM] * 4,
        [array(3 * 1024), array(1024)],
        [
            pltpu.VMEM((3 * 1024, 128), F32),
            pltpu.VMEM((1024, 128), F32),
            pltpu.SemaphoreType.DMA((4,)),
        ],
        "velocity",
        HBM,
    )(*geometry, sums, field, image, pred)
    return velocity.reshape(3, 4, 4, 4, 4, 4, 128), pressure.reshape(4, 4, 4, 4, 4, 128)


def solution(mesh):
    in_specs = (
        P(None, None, None, ("stream", "azim")),
        P(("stream", "azim")),
        P(),
        P(),
        P(),
        P("stream", "azim", None),
    )
    out_specs = (
        P(None, None, None, None, "stream", "azim", None),
        P(None, None, None, "stream", "azim", None),
    )
    return jax.shard_map(body, mesh=mesh, in_specs=in_specs, out_specs=out_specs, check_vma=False)
```
